512 devices in a mesh: wide: 64 (over z, y), narrow: 8 (over x, core).
Axes of the slice: x: 4, y: 4, z: 16, core: 2. Of those that a mesh axis runs over, the one named last changes fastest.
Arguments:
- density: bfloat16 [1024, 64, 2048], P('wide', 'narrow'), may hold values from 0 to 1
- color_table: bfloat16 [3, 256], replicated, may hold values from 0 to 1
- opacity_table: bfloat16 [256], replicated, may hold values from 9.760261e-07 to 0.01953125
- view_shear: int32 [1], replicated, may hold values from -512 to 512
Outputs:
- image: float32 [4, 64, 2048], P(None, 'narrow', 'wide')
The draws below stay inside these ranges and needn't reach their ends.
All inputs are finite; a program needn't handle non-finite values.
Results may differ from the reference program's by a relative error of at most 0.0003.
Values may be sent and summed in bfloat16 or wider, within the bound.
No kernel may reach another device: no remote copies, remote signals or barrier semaphores. Data moves between devices by JAX's collectives and lax.ppermute only.
A program may use at most 64 MiB of HBM per device.

```python
import math
import jax
import jax.numpy as jnp
from jax import lax

NX = 2048
LEVELS = 256
NZ = 1024
NY = 64


def levels(stream_key, shape, shards, smallest, high):
    level, own = 1.0, jax.random.fold_in(stream_key, 6)
    for position, shards_of in shards:
        draws = jnp.exp(jax.random.uniform(jax.random.fold_in(own, position), (shards_of,), jnp.float32, smallest / len(shards), high / len(shards)))
        level = level * jnp.repeat(draws, shape[position] // shards_of).reshape([-1 if axis == position else 1 for axis in range(len(shape))])
    return level


def setup_inputs(seed: int = 0) -> dict:
    seeds = jax.random.split(jax.random.key(seed), 5)
    density = jnp.clip(1.0 * jax.random.uniform(seeds[0], (NZ, NY, NX), jnp.float32) ** levels(seeds[0], (NZ, NY, NX), ((0, 64), (1, 8)), -0.2, 0.2), 0.0, 1.0).astype(jnp.bfloat16)
    color_table = jnp.clip(jax.random.uniform(seeds[1], (3, LEVELS), jnp.float32, 0.0, 1.0), 0.0, 1.0).astype(jnp.bfloat16)
    opacity_table = jnp.clip(jnp.exp(jax.random.uniform(seeds[2], (LEVELS,), jnp.float32, math.log(9.760260581970215e-07), math.log(0.01953125))), 9.760260581970215e-07, 0.01953125).astype(jnp.bfloat16)
    view_shear = jax.random.randint(seeds[3], (1,), 0 - NX // 4, NX // 4 + 1).astype(jnp.int32)
    return dict(density=density, color_table=color_table, opacity_table=opacity_table, view_shear=view_shear)


light_across = 0.48
light_down = 0.6
light_depth = 0.64


def shade_slice(layers, lookup):
    middle = layers[1, 1:-1]
    widened = jnp.pad(middle, ((0, 0), (1, 1)))
    slope_across = 0.5 * (widened[:, 2:] - widened[:, :-2])
    slope_down = 0.5 * (layers[1, 2:] - layers[1, :-2])
    slope_depth = 0.5 * (layers[2, 1:-1] - layers[0, 1:-1])
    facing = light_across * slope_across + light_down * slope_down + light_depth * slope_depth
    strength = slope_across * slope_across + slope_down * slope_down + slope_depth * slope_depth + 0.05
    shading = 0.3 + 0.7 * facing * facing / strength
    scaled = middle * 255.0
    floor_level = jnp.clip(jnp.floor(scaled), 0.0, 254.0)
    fraction = scaled - floor_level
    low_values, high_values = lookup(floor_level)
    sampled = low_values + fraction * (high_values - low_values)
    opacity = sampled[3]
    premult = sampled[:3] * shading * opacity
    return jnp.concatenate([premult, opacity[None]], 0)


def resample(plane_values, slice_global, depth_total, shear_value):
    numerator = shear_value * (2 * slice_global + 1 - depth_total)
    denominator = 2 * depth_total
    whole_shift = jnp.floor_divide(numerator, denominator).astype(jnp.int32)
    offset = (numerator - whole_shift * denominator).astype(jnp.float32) / denominator
    column_count = plane_values.shape[2]
    margin = column_count // 2
    widened = jnp.pad(plane_values, ((0, 0), (0, 0), (margin, margin)))
    aligned = lax.dynamic_slice_in_dim(widened, (margin - whole_shift).astype(jnp.int32), column_count, 2)
    earlier = lax.dynamic_slice_in_dim(widened, (margin - whole_shift - 1).astype(jnp.int32), column_count, 2)
    return offset * earlier + (1.0 - offset) * aligned


def reference(density, color_table, opacity_table, view_shear):
    depth_total, row_count, column_count = density.shape
    lookup_table = jnp.concatenate([color_table, opacity_table[None]], 0).astype(jnp.float32)
    padded = jnp.pad(density, ((1, 1), (1, 1), (0, 0)))
    shear_value = view_shear[0]
    flip_on = jnp.remainder(shear_value, 2).astype(jnp.int32)

    def lookup(floor_level):
        level_index = floor_level.astype(jnp.int32)
        return jnp.take(lookup_table, level_index, axis=1), jnp.take(lookup_table, level_index + 1, axis=1)

    def advance(carried, counter):
        premult_sum, transmit = carried
        slice_global = jnp.where(flip_on == 1, depth_total - 1 - counter, counter).astype(jnp.int32)
        layers = lax.dynamic_slice_in_dim(padded, slice_global, 3, 0).astype(jnp.float32)
        plane_values = resample(shade_slice(layers, lookup), slice_global, depth_total, shear_value)
        return (premult_sum + transmit * plane_values[:3], transmit * (1.0 - plane_values[3])), None

    starting = (jnp.zeros((3, row_count, column_count), jnp.float32), jnp.ones((row_count, column_count), jnp.float32))
    finished, ignored = lax.scan(advance, starting, jnp.arange(depth_total, dtype=jnp.int32))
    premult_sum, transmit = finished
    return jnp.concatenate([premult_sum, (1.0 - transmit)[None]], 0)
```

```python
import functools

import jax
import jax.numpy as jnp
from jax import lax
from jax.experimental import pallas as pl
from jax.experimental.pallas import tpu as pltpu
from jax.sharding import Mesh, PartitionSpec as P

LANES = 128
LEFT = 3
RIGHT = 2
UNROLL = 4
OUTSIDE = -1.0 / 512
LIMIT = 12 * 1024 * 1024


def lane_ids():
    return lax.broadcasted_iota(jnp.int32, (8, LANES), 1)


def row_ids():
    return lax.broadcasted_iota(jnp.int32, (8, LANES), 0)


def pick(table, index):
    return jnp.take_along_axis(table, index, axis=1, mode="promise_in_bounds")


def tile(t):
    return pl.ds(t * LANES, LANES)


def shift_of(shear, z, depth_total):
    numerator = shear * (2 * z + 1 - depth_total)
    denominator = 2 * depth_total
    bits = denominator.bit_length() - 1
    whole = lax.shift_right_arithmetic(numerator, bits)
    rest = numerator - lax.shift_left(whole, bits)
    return whole, rest.astype(jnp.float32) * (1.0 / denominator)


def split_shift(whole):
    hop = lax.shift_right_arithmetic(whole, 7)
    return hop, whole & 127


def next_lane(left, here, lanes):
    return jnp.where(lanes == 0, pltpu.roll(left, 1, 1), pltpu.roll(here, 1, 1))


def lookup_kernel(shear_ref, dens_ref, color_ref, opacity_ref,
                  sample_ref, front_ref, back_ref, alpha_ref, across_ref, deep_ref, down_ref,
                  field_ref, value_ref, opaque_ref, ahead_ref, *, depth_total, place):
    depth, rows, columns = dens_ref.shape
    tiles = columns // LANES
    lanes = lane_ids()
    rows8 = row_ids()
    shear = shear_ref[0]
    start = place() * depth
    flip = (shear & 1) == 1
    zero = jnp.zeros((8, LANES), jnp.float32)
    outside = jnp.full((8, LANES), OUTSIDE, jnp.float32)

    def widen(z, carry):
        for t in range(LEFT):
            field_ref[z, :, tile(t)] = outside
        for t in range(RIGHT):
            field_ref[z, :, tile(LEFT + tiles + t)] = outside
        field_ref[z, :, pl.ds(LEFT * LANES, columns)] = dens_ref[z].astype(jnp.float32)
        return carry

    lax.fori_loop(0, depth, widen, 0)

    def align(i, carry):
        for j in range(UNROLL):
            z = i * UNROLL + j
            whole, g = shift_of(shear, start + z, depth_total)
            hop, r = split_shift(whole)
            base = pl.multiple_of((1 - hop) * LANES, LANES)
            keep = lanes >= r
            rolled = [pltpu.roll(field_ref[z, :, pl.ds(base + t * LANES, LANES)], r, 1) for t in range(tiles + 2)]
            for t in range(tiles + 1):
                value_ref[z, :, tile(t)] = jnp.where(keep, rolled[t + 1], rolled[t])
        return carry

    lax.fori_loop(0, depth // UNROLL, align, 0)

    evens, odds = [], []
    half = (2 * lanes) & 127
    low = lanes < 64
    for c in range(4):
        row = (color_ref[c:c + 1, :] if c < 3 else opacity_ref[...]).astype(jnp.float32)
        first = jnp.broadcast_to(row[:, :LANES], (8, LANES))
        second = jnp.broadcast_to(row[:, LANES:], (8, LANES))
        evens.append(jnp.where(low, pick(first, half), pick(second, half)))
        odds.append(jnp.where(low, pick(first, half + 1), pick(second, half + 1)))

    def sample(z, carry):
        for t in range(tiles + 1):
            value = value_ref[z, :, tile(t)]
            scaled = value * 255.0
            level = jnp.minimum(scaled.astype(jnp.int32), 254)
            even = lax.shift_right_logical(level + 1, 1)
            odd = lax.shift_right_logical(level, 1)
            weight = jnp.abs(scaled - (2 * even).astype(jnp.float32))
            mixed = []
            for c in range(4):
                e = pick(evens[c], even)
                mixed.append(e + weight * (pick(odds[c], odd) - e))
            opacity = jnp.where(value >= 0.0, mixed[3], 0.0)
            for c in range(3):
                sample_ref[c, z, :, tile(t)] = mixed[c] * opacity
            opaque_ref[z, :, tile(t)] = opacity
        return carry

    lax.fori_loop(0, depth, sample, 0)

    for t in range(tiles + 1):
        alpha_ref[:, tile(t)] = zero
        ahead_ref[:, tile(t)] = zero

    def advance(i, carry):
        for j in range(UNROLL):
            step = i * UNROLL + j
            z = jnp.where(flip, depth - 1 - step, step)
            whole, g = shift_of(shear, start + z, depth_total)
            opaque = [opaque_ref[z, :, tile(t)] for t in range(tiles + 1)]
            later = [pltpu.roll(v, 1, 1) for v in opaque]
            sooner = [pltpu.roll(v, LANES - 1, 1) for v in opaque] + [zero]
            for t in range(tiles + 1):
                right = jnp.where(lanes == LANES - 1, sooner[t + 1], sooner[t])
                ahead = ahead_ref[:, tile(t)]
                through = 1.0 - ahead
                front_ref[z, :, tile(t)] = g * through
                ahead_ref[:, tile(t)] = ahead + through * (right + g * (opaque[t] - right))
                if t:
                    left = jnp.where(lanes == 0, later[t - 1], later[t])
                    alpha = alpha_ref[:, tile(t)]
                    through = 1.0 - alpha
                    back_ref[z, :, tile(t)] = through - g * through
                    alpha_ref[:, tile(t)] = alpha + through * (opaque[t] + g * (left - opaque[t]))
                else:
                    back_ref[z, :, tile(t)] = zero
        return carry

    lax.fori_loop(0, depth // UNROLL, advance, 0)

    def slopes(i, carry):
        for j in range(UNROLL):
            z = i * UNROLL + j
            before = lax.max(z - 1, 0)
            after = lax.min(z + 1, depth - 1)
            inner_low = jnp.where(z > 0, 1.0, 0.0)
            inner_high = jnp.where(z < depth - 1, 1.0, 0.0)
            slabs = [field_ref[z, :, tile(LEFT + t)] for t in range(tiles)]
            later = [zero] + [pltpu.roll(v, 1, 1) for v in slabs]
            sooner = [pltpu.roll(v, LANES - 1, 1) for v in slabs] + [zero]
            for t in range(tiles):
                left = jnp.where(lanes == 0, later[t], later[t + 1])
                right = jnp.where(lanes == LANES - 1, sooner[t + 1], sooner[t])
                below = jnp.where(rows8 == 7, 0.0, pltpu.roll(slabs[t], 7, 0))
                above = jnp.where(rows8 == 0, 0.0, pltpu.roll(slabs[t], 1, 0))
                across_ref[z, :, tile(t)] = right - left
                down_ref[z, :, tile(t)] = below - above
                deep_ref[z, :, tile(t)] = (inner_high * field_ref[after, :, tile(LEFT + t)]
                                           - inner_low * field_ref[before, :, tile(LEFT + t)])
        return carry

    lax.fori_loop(0, depth // UNROLL, slopes, 0)


def shade_kernel(shear_ref, sample_ref, front_ref, back_ref, alpha_ref, across_ref, deep_ref, down_ref,
                 lo_ref, hi_ref, dn_ref, up_ref,
                 out_ref, shade_ref, moved_ref, above_ref, below_ref, now_ref, late_ref, *, depth_total, place):
    depth, rows, columns = across_ref.shape
    tiles = columns // LANES
    lanes = lane_ids()
    rows8 = row_ids()
    shear = shear_ref[0]
    start = place() * depth
    zero = jnp.zeros((8, LANES), jnp.float32)

    above_ref[...] = -dn_ref[...].astype(jnp.float32)
    below_ref[...] = up_ref[...].astype(jnp.float32)
    for z in range(depth):
        for t in range(LEFT):
            shade_ref[z, :, tile(t)] = zero
        for t in range(RIGHT):
            shade_ref[z, :, tile(LEFT + tiles + t)] = zero

    def shade(t, carry):
        here = pl.ds(pl.multiple_of(t * LANES, LANES), LANES)
        there = pl.ds(pl.multiple_of((t + LEFT) * LANES, LANES), LANES)
        for z in range(depth):
            above = jnp.broadcast_to(above_ref[z:z + 1, here], (8, LANES))
            below = jnp.broadcast_to(below_ref[z:z + 1, here], (8, LANES))
            extra = jnp.where(rows8 == 0, above, jnp.where(rows8 == 7, below, 0.0))
            down = down_ref[z, :, here] + extra
            deep = deep_ref[z, :, here]
            if z == 0:
                deep = deep - lo_ref[:, here].astype(jnp.float32)
            if z == depth - 1:
                deep = deep + hi_ref[:, here].astype(jnp.float32)
            across = across_ref[z, :, here]
            facing = 0.48 * across + 0.6 * down + 0.64 * deep
            strength = across * across + down * down + (deep * deep + 0.2)
            shade_ref[z, :, there] = 0.3 + 0.7 * facing * facing / strength
        return carry

    lax.fori_loop(0, tiles, shade, 0)

    def align(i, carry):
        for j in range(UNROLL):
            z = i * UNROLL + j
            whole, g = shift_of(shear, start + z, depth_total)
            hop, r = split_shift(whole)
            base = pl.multiple_of((1 - hop) * LANES, LANES)
            keep = lanes >= r
            rolled = [pltpu.roll(shade_ref[z, :, pl.ds(base + t * LANES, LANES)], r, 1) for t in range(tiles + 2)]
            for t in range(tiles + 1):
                moved_ref[z, :, tile(t)] = jnp.where(keep, rolled[t + 1], rolled[t])
        return carry

    lax.fori_loop(0, depth // UNROLL, align, 0)

    def gather(t, carry):
        here = pl.ds(pl.multiple_of(t * LANES, LANES), LANES)
        late = [zero] * 3
        now = [zero] * 3
        for z in range(depth):
            shading = moved_ref[z, :, here]
            front = front_ref[z, :, here] * shading
            back = back_ref[z, :, here] * shading
            for c in range(3):
                value = sample_ref[c, z, :, here]
                late[c] = late[c] + front * value
                now[c] = now[c] + back * value
        for c in range(3):
            late_ref[c, :, here] = late[c]
            now_ref[c, :, here] = now[c]
        return carry

    lax.fori_loop(0, tiles + 1, gather, 0)

    quarter = lax.shift_right_logical(lanes, 5)
    late = [[pltpu.roll(late_ref[c, :, tile(t)], 1, 1) for t in range(tiles + 1)] for c in range(3)]
    for t in range(tiles):
        parts = [now_ref[c, :, tile(t + 1)] + jnp.where(lanes == 0, late[c][t], late[c][t + 1]) for c in range(3)]
        parts.append(alpha_ref[:, tile(t + 1)])
        for y in range(4):
            moved = [parts[c] if c == y else pltpu.roll(parts[c], (32 * (c - y)) % LANES, 1) for c in range(4)]
            out_ref[4 * t + y] = jnp.where(quarter < 2, jnp.where(quarter == 0, moved[0], moved[1]),
                                           jnp.where(quarter == 2, moved[2], moved[3]))


def merge_kernel(shear_ref, parts_ref, out_ref):
    count = parts_ref.shape[0]
    lanes = lane_ids()
    flip = (shear_ref[0] & 1) == 1
    owner = 96 + (lanes & 31)
    total = jnp.zeros((8, LANES), jnp.float32)
    through = jnp.ones((8, LANES), jnp.float32)
    for i in range(count):
        block = parts_ref[jnp.where(flip, count - 1 - i, i)]
        total = total + through * block
        through = through - through * pick(block, owner)
    for c in range(4):
        out_ref[c] = total[:, 32 * c:32 * c + 32]


def per_device(density, color_table, opacity_table, view_shear, place=None, halos=None):
    depth, rows, columns = density.shape
    wide = 64
    depth_total = depth * wide
    if place is None:
        place = lambda: lax.axis_index("wide")
    f32 = jnp.float32
    vmem = pl.BlockSpec(memory_space=pltpu.VMEM)
    smem = pl.BlockSpec(memory_space=pltpu.SMEM)
    if halos is None:
        up_wide = [(i, i + 1) for i in range(wide - 1)]
        down_wide = [(b, a) for a, b in up_wide]
        up_narrow = [(i, i + 1) for i in range(7)]
        down_narrow = [(b, a) for a, b in up_narrow]
        lo = lax.ppermute(density[-1], "wide", up_wide)
        hi = lax.ppermute(density[0], "wide", down_wide)
        dn = lax.ppermute(density[:, -1], "narrow", up_narrow)
        up = lax.ppermute(density[:, 0], "narrow", down_narrow)
    else:
        lo, hi, dn, up = halos
    slab = (depth, rows, columns)
    wider = (depth, rows, columns + LANES)
    widest = (depth, rows, columns + (LEFT + RIGHT) * LANES)
    row = (rows, columns + LANES)
    local = pl.pallas_call(
        functools.partial(lookup_kernel, depth_total=depth_total, place=place),
        in_specs=[smem, vmem, vmem, vmem],
        out_specs=[vmem] * 7,
        out_shape=[pltpu.VMEM((3,) + wider, f32), pltpu.VMEM(wider, f32), pltpu.VMEM(wider, f32), pltpu.VMEM(row, f32),
                   pltpu.VMEM(slab, f32), pltpu.VMEM(slab, f32), pltpu.VMEM(slab, f32)],
        scratch_shapes=[pltpu.VMEM(widest, f32), pltpu.VMEM(wider, f32), pltpu.VMEM(wider, f32), pltpu.VMEM(row, f32)],
        compiler_params=pltpu.CompilerParams(vmem_limit_bytes=LIMIT),
        cost_estimate=pl.CostEstimate(flops=30_000_000, bytes_accessed=10_000_000, transcendentals=0),
        name="lookup",
    )(view_shear, density, color_table, opacity_table[None])
    bricks = pl.pallas_call(
        functools.partial(shade_kernel, depth_total=depth_total, place=place),
        in_specs=[smem] + [vmem] * 11,
        out_specs=vmem,
        out_shape=jax.ShapeDtypeStruct((wide, rows, LANES), f32),
        scratch_shapes=[pltpu.VMEM(widest, f32), pltpu.VMEM(wider, f32), pltpu.VMEM((depth, columns), f32),
                        pltpu.VMEM((depth, columns), f32), pltpu.VMEM((3,) + row, f32), pltpu.VMEM((3,) + row, f32)],
        compiler_params=pltpu.CompilerParams(vmem_limit_bytes=LIMIT),
        name="shade",
    )(view_shear, *local, lo, hi, dn, up)
    if halos is not None:
        return bricks
    parts = lax.all_to_all(bricks, "wide", split_axis=0, concat_axis=0, tiled=True)
    return pl.pallas_call(
        merge_kernel,
        in_specs=[smem, vmem],
        out_specs=vmem,
        out_shape=jax.ShapeDtypeStruct((4, rows, 32), f32),
        name="merge",
    )(view_shear, parts)


def solution(mesh):
    placed = (P("wide", "narrow", None), P(), P(), P())
    return jax.shard_map(
        per_device, mesh=mesh, in_specs=placed, out_specs=P(None, "narrow", "wide"), check_vma=False
    )
```

```python
import functools

import jax
import jax.numpy as jnp
from jax import lax
from jax.experimental import pallas as pl
from jax.experimental.pallas import tpu as pltpu
from jax.sharding import Mesh, PartitionSpec as P

LANES = 128
LEFT = 3
RIGHT = 2
UNROLL = 4
FEW = 4
OUTSIDE = -1.0 / 512
RATIO_STEPS = 65000.0
LOG_SPAN = 26.0
LOG_STEPS = 65534.0 / (LOG_SPAN - 1.85)
TINY = 1e-12
LIMIT = 12 * 1024 * 1024


def lane_ids():
    return lax.broadcasted_iota(jnp.int32, (8, LANES), 1)


def row_ids():
    return lax.broadcasted_iota(jnp.int32, (8, LANES), 0)


def pick(table, index):
    return jnp.take_along_axis(table, index, axis=1, mode="promise_in_bounds")


def tile(t):
    return pl.ds(t * LANES, LANES)


def shift_of(shear, z, depth_total):
    numerator = shear * (2 * z + 1 - depth_total)
    denominator = 2 * depth_total
    bits = denominator.bit_length() - 1
    whole = lax.shift_right_arithmetic(numerator, bits)
    rest = numerator - lax.shift_left(whole, bits)
    return whole, rest.astype(jnp.float32) * (1.0 / denominator)


def split_shift(whole):
    hop = lax.shift_right_arithmetic(whole, 7)
    return hop, whole & 127


def next_lane(left, here, lanes):
    return jnp.where(lanes == 0, pltpu.roll(left, 1, 1), pltpu.roll(here, 1, 1))


def phase(place):
    return ((place * 39) & 63) * (1.0 / 64.0) if isinstance(place, int) else ((place * 39) & 63).astype(jnp.float32) * (1.0 / 64.0)


def encode(colors, alpha, offset):
    inverse = RATIO_STEPS / jnp.maximum(alpha, TINY)
    parts = [jnp.minimum(c * inverse + 0.5, 65535.0) for c in colors]
    level = jnp.log2(jnp.maximum(alpha, TINY)) * LOG_STEPS + (LOG_SPAN * LOG_STEPS + offset)
    parts.append(jnp.clip(level, 0.0, 65535.0))
    return [p.astype(jnp.int32) - 32768 for p in parts]


def decode(codes, lanes, owner, offset):
    value = codes.astype(jnp.int32).astype(jnp.float32) + 32768.0
    level = pick(value, owner)
    alpha = jnp.exp2((level + (0.5 - offset)) * (1.0 / LOG_STEPS) - LOG_SPAN)
    alpha = jnp.where(level > 0.0, alpha, 0.0)
    return alpha, alpha * jnp.where(lanes < 96, value * (1.0 / RATIO_STEPS), 1.0)


def lookup_kernel(shear_ref, dens_ref, color_ref, opacity_ref,
                  sample_ref, front_ref, back_ref, alpha_ref, across_ref, deep_ref, down_ref,
                  field_ref, value_ref, opaque_ref, ahead_ref, *, depth_total, place):
    depth, rows, columns = dens_ref.shape
    tiles = columns // LANES
    lanes = lane_ids()
    rows8 = row_ids()
    shear = shear_ref[0]
    start = place() * depth
    flip = (shear & 1) == 1
    zero = jnp.zeros((8, LANES), jnp.float32)
    outside = jnp.full((8, LANES), OUTSIDE, jnp.float32)

    def widen(z, carry):
        for t in range(LEFT):
            field_ref[z, :, tile(t)] = outside
        for t in range(RIGHT):
            field_ref[z, :, tile(LEFT + tiles + t)] = outside
        field_ref[z, :, pl.ds(LEFT * LANES, columns)] = dens_ref[z].astype(jnp.float32)
        return carry

    lax.fori_loop(0, depth, widen, 0)

    def align(i, carry):
        for j in range(UNROLL):
            z = i * UNROLL + j
            whole, g = shift_of(shear, start + z, depth_total)
            hop, r = split_shift(whole)
            base = pl.multiple_of((1 - hop) * LANES, LANES)
            keep = lanes >= r
            rolled = [pltpu.roll(field_ref[z, :, pl.ds(base + t * LANES, LANES)], r, 1) for t in range(tiles + 2)]
            for t in range(tiles + 1):
                value_ref[z, :, tile(t)] = jnp.where(keep, rolled[t + 1], rolled[t])
        return carry

    lax.fori_loop(0, depth // UNROLL, align, 0)

    evens, odds = [], []
    half = (2 * lanes) & 127
    low = lanes < 64
    for c in range(4):
        row = (color_ref[c:c + 1, :] if c < 3 else opacity_ref[...].reshape(1, -1)).astype(jnp.float32)
        first = jnp.broadcast_to(row[:, :LANES], (8, LANES))
        second = jnp.broadcast_to(row[:, LANES:], (8, LANES))
        evens.append(jnp.where(low, pick(first, half), pick(second, half)))
        odds.append(jnp.where(low, pick(first, half + 1), pick(second, half + 1)))

    def sample(i, carry):
        for z, t in [(i * FEW + j, t) for j in range(FEW) for t in range(tiles + 1)]:
            value = value_ref[z, :, tile(t)]
            scaled = value * 255.0
            level = jnp.minimum(scaled.astype(jnp.int32), 254)
            even = lax.shift_right_logical(level + 1, 1)
            odd = lax.shift_right_logical(level, 1)
            weight = jnp.abs(scaled - (2 * even).astype(jnp.float32))
            lower = [pick(table, even) for table in evens]
            upper = [pick(table, odd) for table in odds]
            mixed = [e + weight * (o - e) for e, o in zip(lower, upper)]
            opacity = jnp.where(value >= 0.0, mixed[3], 0.0)
            for c in range(3):
                sample_ref[c, z, :, tile(t)] = mixed[c] * opacity
            opaque_ref[z, :, tile(t)] = opacity
        return carry

    lax.fori_loop(0, depth // FEW, sample, 0)

    for t in range(tiles + 1):
        alpha_ref[:, tile(t)] = zero
        ahead_ref[:, tile(t)] = zero

    def advance(i, carry):
        for j in range(UNROLL):
            step = i * UNROLL + j
            z = jnp.where(flip, depth - 1 - step, step)
            whole, g = shift_of(shear, start + z, depth_total)
            opaque = [opaque_ref[z, :, tile(t)] for t in range(tiles + 1)]
            later = [pltpu.roll(v, 1, 1) for v in opaque]
            sooner = [pltpu.roll(v, LANES - 1, 1) for v in opaque] + [zero]
            for t in range(tiles + 1):
                right = jnp.where(lanes == LANES - 1, sooner[t + 1], sooner[t])
                ahead = ahead_ref[:, tile(t)]
                through = 1.0 - ahead
                front_ref[z, :, tile(t)] = g * through
                ahead_ref[:, tile(t)] = ahead + through * (right + g * (opaque[t] - right))
                if t:
                    left = jnp.where(lanes == 0, later[t - 1], later[t])
                    alpha = alpha_ref[:, tile(t)]
                    through = 1.0 - alpha
                    back_ref[z, :, tile(t)] = through - g * through
                    alpha_ref[:, tile(t)] = alpha + through * (opaque[t] + g * (left - opaque[t]))
                else:
                    back_ref[z, :, tile(t)] = zero
        return carry

    lax.fori_loop(0, depth // UNROLL, advance, 0)

    def slopes(i, carry):
        for j in range(UNROLL):
            z = i * UNROLL + j
            before = lax.max(z - 1, 0)
            after = lax.min(z + 1, depth - 1)
            inner_low = jnp.where(z > 0, 1.0, 0.0)
            inner_high = jnp.where(z < depth - 1, 1.0, 0.0)
            slabs = [field_ref[z, :, tile(LEFT + t)] for t in range(tiles)]
            later = [zero] + [pltpu.roll(v, 1, 1) for v in slabs]
            sooner = [pltpu.roll(v, LANES - 1, 1) for v in slabs] + [zero]
            for t in range(tiles):
                left = jnp.where(lanes == 0, later[t], later[t + 1])
                right = jnp.where(lanes == LANES - 1, sooner[t + 1], sooner[t])
                below = jnp.where(rows8 == 7, 0.0, pltpu.roll(slabs[t], 7, 0))
                above = jnp.where(rows8 == 0, 0.0, pltpu.roll(slabs[t], 1, 0))
                across_ref[z, :, tile(t)] = right - left
                down_ref[z, :, tile(t)] = below - above
                deep_ref[z, :, tile(t)] = (inner_high * field_ref[after, :, tile(LEFT + t)]
                                           - inner_low * field_ref[before, :, tile(LEFT + t)])
        return carry

    lax.fori_loop(0, depth // UNROLL, slopes, 0)


def shade_kernel(shear_ref, sample_ref, front_ref, back_ref, alpha_ref, across_ref, deep_ref, down_ref,
                 slice_a_ref, slice_b_ref, row_a_ref, row_b_ref,
                 out_ref, shade_ref, moved_ref, above_ref, below_ref, now_ref, late_ref, *, depth_total, place, across):
    depth, rows, columns = across_ref.shape
    tiles = columns // LANES
    lanes = lane_ids()
    rows8 = row_ids()
    shear = shear_ref[0]
    start = place() * depth
    zero = jnp.zeros((8, LANES), jnp.float32)

    wide_odd = (place() & 1) == 1
    narrow_odd = (across() & 1) == 1
    row_a = row_a_ref[...].astype(jnp.float32)
    row_b = row_b_ref[...].astype(jnp.float32)
    above_ref[...] = -jnp.where(narrow_odd, row_a, row_b)
    below_ref[...] = jnp.where(narrow_odd, row_b, row_a)
    for z in range(depth):
        for t in range(LEFT):
            shade_ref[z, :, tile(t)] = zero
        for t in range(RIGHT):
            shade_ref[z, :, tile(LEFT + tiles + t)] = zero

    def shade(t, carry):
        here = pl.ds(pl.multiple_of(t * LANES, LANES), LANES)
        there = pl.ds(pl.multiple_of((t + LEFT) * LANES, LANES), LANES)
        for z in range(depth):
            above = jnp.broadcast_to(above_ref[z:z + 1, here], (8, LANES))
            below = jnp.broadcast_to(below_ref[z:z + 1, here], (8, LANES))
            extra = jnp.where(rows8 == 0, above, jnp.where(rows8 == 7, below, 0.0))
            down = down_ref[z, :, here] + extra
            deep = deep_ref[z, :, here]
            if z == 0 or z == depth - 1:
                slice_a = slice_a_ref[:, here].astype(jnp.float32)
                slice_b = slice_b_ref[:, here].astype(jnp.float32)
                if z == 0:
                    deep = deep - jnp.where(wide_odd, slice_a, slice_b)
                else:
                    deep = deep + jnp.where(wide_odd, slice_b, slice_a)
            side = across_ref[z, :, here]
            facing = 0.48 * side + 0.6 * down + 0.64 * deep
            strength = side * side + down * down + (deep * deep + 0.2)
            shade_ref[z, :, there] = 0.3 + 0.7 * facing * facing / strength
        return carry

    lax.fori_loop(0, tiles, shade, 0)

    def align(i, carry):
        for j in range(UNROLL):
            z = i * UNROLL + j
            whole, g = shift_of(shear, start + z, depth_total)
            hop, r = split_shift(whole)
            base = pl.multiple_of((1 - hop) * LANES, LANES)
            keep = lanes >= r
            rolled = [pltpu.roll(shade_ref[z, :, pl.ds(base + t * LANES, LANES)], r, 1) for t in range(tiles + 2)]
            for t in range(tiles + 1):
                moved_ref[z, :, tile(t)] = jnp.where(keep, rolled[t + 1], rolled[t])
        return carry

    lax.fori_loop(0, depth // UNROLL, align, 0)

    def gather(t, carry):
        here = pl.ds(pl.multiple_of(t * LANES, LANES), LANES)
        late = [zero] * 3
        now = [zero] * 3
        for z in range(depth):
            shading = moved_ref[z, :, here]
            front = front_ref[z, :, here] * shading
            back = back_ref[z, :, here] * shading
            for c in range(3):
                value = sample_ref[c, z, :, here]
                late[c] = late[c] + front * value
                now[c] = now[c] + back * value
        for c in range(3):
            late_ref[c, :, here] = late[c]
            now_ref[c, :, here] = now[c]
        return carry

    lax.fori_loop(0, tiles + 1, gather, 0)

    quarter = lax.shift_right_logical(lanes, 5)
    late = [[pltpu.roll(late_ref[c, :, tile(t)], 1, 1) for t in range(tiles + 1)] for c in range(3)]
    for t in range(tiles):
        parts = [now_ref[c, :, tile(t + 1)] + jnp.where(lanes == 0, late[c][t], late[c][t + 1]) for c in range(3)]
        parts = encode(parts, alpha_ref[:, tile(t + 1)], phase(place()))
        for y in range(4):
            moved = [parts[c] if c == y else pltpu.roll(parts[c], (32 * (c - y)) % LANES, 1) for c in range(4)]
            block = jnp.where(quarter < 2, jnp.where(quarter == 0, moved[0], moved[1]),
                              jnp.where(quarter == 2, moved[2], moved[3]))
            out_ref[4 * t + y] = block.astype(jnp.int16)


def merge_kernel(shear_ref, parts_ref, out_ref):
    count = parts_ref.shape[0]
    lanes = lane_ids()
    flip = (shear_ref[0] & 1) == 1
    owner = 96 + (lanes & 31)
    total = jnp.zeros((8, LANES), jnp.float32)
    through = jnp.ones((8, LANES), jnp.float32)
    for i in range(count):
        slot = jnp.where(flip, count - 1 - i, i)
        alpha, value = decode(parts_ref[slot], lanes, owner, phase(slot))
        total = total + through * value
        through = through - through * alpha
    for c in range(4):
        out_ref[c] = total[:, 32 * c:32 * c + 32]


def pairs(count, start):
    return [p for i in range(start, count - 1, 2) for p in ((i, i + 1), (i + 1, i))]


def per_device(density, color_table, opacity_table, view_shear, place=None, across=None, halos=None):
    depth, rows, columns = density.shape
    wide = 64
    depth_total = depth * wide
    if place is None:
        place = lambda: lax.axis_index("wide")
        across = lambda: lax.axis_index("narrow")
    f32 = jnp.float32
    vmem = pl.BlockSpec(memory_space=pltpu.VMEM)
    smem = pl.BlockSpec(memory_space=pltpu.SMEM)
    if halos is None:
        wide_odd = (lax.axis_index("wide") & 1) == 1
        narrow_odd = (lax.axis_index("narrow") & 1) == 1
        first, last = density[:, 0], density[:, -1]
        row_a = lax.ppermute(jnp.where(narrow_odd, first, last), "narrow", pairs(8, 0))
        row_b = lax.ppermute(jnp.where(narrow_odd, last, first), "narrow", pairs(8, 1))
        first, last = density[0], density[-1]
        slice_a = lax.ppermute(jnp.where(wide_odd, first, last), "wide", pairs(wide, 0))
        slice_b = lax.ppermute(jnp.where(wide_odd, last, first), "wide", pairs(wide, 1))
    else:
        slice_a, slice_b, row_a, row_b = halos
    slab = (depth, rows, columns)
    wider = (depth, rows, columns + LANES)
    widest = (depth, rows, columns + (LEFT + RIGHT) * LANES)
    row = (rows, columns + LANES)
    local = pl.pallas_call(
        functools.partial(lookup_kernel, depth_total=depth_total, place=place),
        in_specs=[smem, vmem, vmem, vmem],
        out_specs=[vmem] * 7,
        out_shape=[pltpu.VMEM((3,) + wider, f32), pltpu.VMEM(wider, f32), pltpu.VMEM(wider, f32), pltpu.VMEM(row, f32),
                   pltpu.VMEM(slab, f32), pltpu.VMEM(slab, f32), pltpu.VMEM(slab, f32)],
        scratch_shapes=[pltpu.VMEM(widest, f32), pltpu.VMEM(wider, f32), pltpu.VMEM(wider, f32), pltpu.VMEM(row, f32)],
        compiler_params=pltpu.CompilerParams(vmem_limit_bytes=LIMIT),
        cost_estimate=pl.CostEstimate(flops=30_000_000, bytes_accessed=10_000_000, transcendentals=0),
        name="lookup",
    )(view_shear, density, color_table, opacity_table)
    bricks = pl.pallas_call(
        functools.partial(shade_kernel, depth_total=depth_total, place=place, across=across),
        in_specs=[smem] + [vmem] * 11,
        out_specs=vmem,
        out_shape=pltpu.VMEM((wide, rows, LANES), jnp.int16),
        scratch_shapes=[pltpu.VMEM(widest, f32), pltpu.VMEM(wider, f32), pltpu.VMEM((depth, columns), f32),
                        pltpu.VMEM((depth, columns), f32), pltpu.VMEM((3,) + row, f32), pltpu.VMEM((3,) + row, f32)],
        compiler_params=pltpu.CompilerParams(vmem_limit_bytes=LIMIT),
        name="shade",
    )(view_shear, *local, slice_a, slice_b, row_a, row_b)
    if halos is not None:
        return bricks
    parts = lax.all_to_all(bricks, "wide", split_axis=0, concat_axis=0, tiled=True)
    return pl.pallas_call(
        merge_kernel,
        in_specs=[smem, vmem],
        out_specs=vmem,
        out_shape=jax.ShapeDtypeStruct((4, rows, 32), f32),
        name="merge",
    )(view_shear, parts)


def solution(mesh):
    placed = (P("wide", "narrow", None), P(), P(), P())
    return jax.shard_map(
        per_device, mesh=mesh, in_specs=placed, out_specs=P(None, "narrow", "wide"), check_vma=False
    )
```

```python
import functools

import jax
import jax.numpy as jnp
from jax import lax
from jax.experimental import pallas as pl
from jax.experimental.pallas import tpu as pltpu
from jax.sharding import Mesh, PartitionSpec as P

LANES = 128
LEFT = 3
RIGHT = 2
UNROLL = 4
FEW = 4
OUTSIDE = -1.0 / 512
RATIO_STEPS = 65000.0
LOG_SPAN = 26.0
LOG_STEPS = 65534.0 / (LOG_SPAN - 1.85)
TINY = 1e-12
TURN = 36
CHUNKS = 4
LIMIT = 12 * 1024 * 1024


def lane_ids():
    return lax.broadcasted_iota(jnp.int32, (8, LANES), 1)


def row_ids():
    return lax.broadcasted_iota(jnp.int32, (8, LANES), 0)


def pick(table, index):
    return jnp.take_along_axis(table, index, axis=1, mode="promise_in_bounds")


def tile(t):
    return pl.ds(t * LANES, LANES)


def shift_of(shear, z, depth_total):
    numerator = shear * (2 * z + 1 - depth_total)
    denominator = 2 * depth_total
    bits = denominator.bit_length() - 1
    whole = lax.shift_right_arithmetic(numerator, bits)
    rest = numerator - lax.shift_left(whole, bits)
    return whole, rest.astype(jnp.float32) * (1.0 / denominator)


def split_shift(whole):
    hop = lax.shift_right_arithmetic(whole, 7)
    return hop, whole & 127


def next_lane(left, here, lanes):
    return jnp.where(lanes == 0, pltpu.roll(left, 1, 1), pltpu.roll(here, 1, 1))


def phase(place):
    return ((place * 39) & 63) * (1.0 / 64.0) if isinstance(place, int) else ((place * 39) & 63).astype(jnp.float32) * (1.0 / 64.0)


def encode(colors, alpha, offset):
    inverse = RATIO_STEPS / jnp.maximum(alpha, TINY)
    parts = [jnp.minimum(c * inverse + 0.5, 65535.0) for c in colors]
    level = jnp.log2(jnp.maximum(alpha, TINY)) * LOG_STEPS + (LOG_SPAN * LOG_STEPS + offset)
    parts.append(jnp.clip(level, 0.0, 65535.0))
    return [p.astype(jnp.int32) - 32768 for p in parts]


def decode(codes, lanes, owner, offset):
    value = codes.astype(jnp.int32).astype(jnp.float32) + 32768.0
    level = pick(value, owner)
    alpha = jnp.exp2((level + (0.5 - offset)) * (1.0 / LOG_STEPS) - LOG_SPAN)
    alpha = jnp.where(level > 0.0, alpha, 0.0)
    return alpha, alpha * jnp.where(lanes < 96, value * (1.0 / RATIO_STEPS), 1.0)


def prepare_kernel(dens_hbm, field_ref, slice_a_ref, slice_b_ref, row_a_ref, row_b_ref,
                   dens_ref, top_ref, bottom_ref, arrived, *, place, across):
    depth, rows, columns = dens_ref.shape
    tiles = columns // LANES
    chunk = depth // CHUNKS
    copies = [pltpu.make_async_copy(dens_hbm.at[pl.ds(i * chunk, chunk)], dens_ref.at[pl.ds(i * chunk, chunk)],
                                    arrived.at[i]) for i in range(CHUNKS)]
    for copy in copies:
        copy.start()
    outside = jnp.full((8, LANES), OUTSIDE, jnp.float32)
    for z in range(depth):
        for t in range(LEFT):
            field_ref[z, :, tile(t)] = outside
        for t in range(RIGHT):
            field_ref[z, :, tile(LEFT + tiles + t)] = outside
    for i in range(CHUNKS):
        copies[i].wait()
        for z in range(i * chunk, (i + 1) * chunk):
            slab = dens_ref[z].astype(jnp.float32)
            field_ref[z, :, pl.ds(LEFT * LANES, columns)] = slab
            top_ref[z:z + 1, :] = slab[:1]
            bottom_ref[z:z + 1, :] = slab[rows - 1:]
    wide_odd = (place() & 1) == 1
    narrow_odd = (across() & 1) == 1
    top, bottom = top_ref[...], bottom_ref[...]
    row_a_ref[...] = jnp.where(narrow_odd, top, bottom).astype(jnp.bfloat16)
    row_b_ref[...] = jnp.where(narrow_odd, bottom, top).astype(jnp.bfloat16)
    first = field_ref[0, :, pl.ds(LEFT * LANES, columns)]
    last = field_ref[depth - 1, :, pl.ds(LEFT * LANES, columns)]
    slice_a_ref[...] = jnp.where(wide_odd, first, last).astype(jnp.bfloat16)
    slice_b_ref[...] = jnp.where(wide_odd, last, first).astype(jnp.bfloat16)


def lookup_kernel(shear_ref, field_ref, color_hbm, opacity_hbm,
                  sample_ref, front_ref, back_ref, alpha_ref, across_ref, deep_ref, down_ref,
                  value_ref, opaque_ref, ahead_ref, color_ref, opacity_ref, arrived, *, depth_total, place):
    depth, rows, columns = across_ref.shape
    tiles = columns // LANES
    lanes = lane_ids()
    rows8 = row_ids()
    shear = shear_ref[0]
    start = place() * depth
    flip = (shear & 1) == 1
    zero = jnp.zeros((8, LANES), jnp.float32)
    copies = [pltpu.make_async_copy(color_hbm, color_ref, arrived.at[0]),
              pltpu.make_async_copy(opacity_hbm, opacity_ref, arrived.at[1])]
    for copy in copies:
        copy.start()

    def align(i, carry):
        for j in range(UNROLL):
            z = i * UNROLL + j
            whole, g = shift_of(shear, start + z, depth_total)
            hop, r = split_shift(whole)
            base = pl.multiple_of((1 - hop) * LANES, LANES)
            keep = lanes >= r
            rolled = [pltpu.roll(field_ref[z, :, pl.ds(base + t * LANES, LANES)], r, 1) for t in range(tiles + 2)]
            for t in range(tiles + 1):
                value_ref[z, :, tile(t)] = jnp.where(keep, rolled[t + 1], rolled[t])
        return carry

    lax.fori_loop(0, depth // UNROLL, align, 0)

    for copy in copies:
        copy.wait()
    evens, odds = [], []
    half = (2 * lanes) & 127
    low = lanes < 64
    for c in range(4):
        row = (color_ref[c:c + 1, :] if c < 3 else opacity_ref[...].reshape(1, -1)).astype(jnp.float32)
        first = jnp.broadcast_to(row[:, :LANES], (8, LANES))
        second = jnp.broadcast_to(row[:, LANES:], (8, LANES))
        evens.append(jnp.where(low, pick(first, half), pick(second, half)))
        odds.append(jnp.where(low, pick(first, half + 1), pick(second, half + 1)))

    def slopes(z):
        if True:
            before = lax.max(z - 1, 0)
            after = lax.min(z + 1, depth - 1)
            inner_low = jnp.where(z > 0, 1.0, 0.0)
            inner_high = jnp.where(z < depth - 1, 1.0, 0.0)
            slabs = [field_ref[z, :, tile(LEFT + t)] for t in range(tiles)]
            later = [zero] + [pltpu.roll(v, 1, 1) for v in slabs]
            sooner = [pltpu.roll(v, LANES - 1, 1) for v in slabs] + [zero]
            for t in range(tiles):
                left = jnp.where(lanes == 0, later[t], later[t + 1])
                right = jnp.where(lanes == LANES - 1, sooner[t + 1], sooner[t])
                below = jnp.where(rows8 == 7, 0.0, pltpu.roll(slabs[t], 7, 0))
                above = jnp.where(rows8 == 0, 0.0, pltpu.roll(slabs[t], 1, 0))
                across_ref[z, :, tile(t)] = right - left
                down_ref[z, :, tile(t)] = below - above
                deep_ref[z, :, tile(t)] = (inner_high * field_ref[after, :, tile(LEFT + t)]
                                           - inner_low * field_ref[before, :, tile(LEFT + t)])

    evens = [(jnp.floor(evens[0] * 32767.0 + 0.5).astype(jnp.int32) * 65536
              + jnp.floor(evens[1] * 65535.0 + 0.5).astype(jnp.int32)), evens[3] + evens[3] * (evens[2] * (1.0 / 512.0))]
    odds = [(jnp.floor(odds[0] * 32767.0 + 0.5).astype(jnp.int32) * 65536
             + jnp.floor(odds[1] * 65535.0 + 0.5).astype(jnp.int32)), odds[3] + odds[3] * (odds[2] * (1.0 / 512.0))]

    def split(word):
        return [lax.shift_right_logical(word, 16).astype(jnp.float32), (word & 65535).astype(jnp.float32)]

    def part(word):
        wide = word * 65537.0
        opacity = wide - (wide - word)
        return [(word - opacity) * pl.reciprocal(opacity, approx=True), opacity]

    def sample(i, carry):
        for j in range(FEW):
            slopes(i * FEW + j)
        for z, t in [(i * FEW + j, t) for j in range(FEW) for t in range(tiles + 1)]:
            value = value_ref[z, :, tile(t)]
            scaled = value * 255.0
            level = jnp.minimum(scaled.astype(jnp.int32), 254)
            even = lax.shift_right_logical(level + 1, 1)
            odd = lax.shift_right_logical(level, 1)
            weight = jnp.abs(scaled - (2 * even).astype(jnp.float32))
            lower = [pick(table, even) for table in evens]
            upper = [pick(table, odd) for table in odds]
            lower = split(lower[0]) + part(lower[1])
            upper = split(upper[0]) + part(upper[1])
            mixed = [e + weight * (o - e) for e, o in zip(lower, upper)]
            opacity = jnp.where(value >= 0.0, mixed[3], 0.0)
            sample_ref[0, z, :, tile(t)] = mixed[0] * (opacity * (1.0 / 32767.0))
            sample_ref[1, z, :, tile(t)] = mixed[1] * (opacity * (1.0 / 65535.0))
            sample_ref[2, z, :, tile(t)] = mixed[2] * (opacity * 512.0)
            opaque_ref[z, :, tile(t)] = opacity
        return carry

    lax.fori_loop(0, depth // FEW, sample, 0)

    for t in range(tiles + 1):
        alpha_ref[:, tile(t)] = zero
        ahead_ref[:, tile(t)] = zero

    def advance(i, carry):
        for j in range(UNROLL):
            step = i * UNROLL + j
            z = jnp.where(flip, depth - 1 - step, step)
            whole, g = shift_of(shear, start + z, depth_total)
            opaque = [opaque_ref[z, :, tile(t)] for t in range(tiles + 1)]
            later = [pltpu.roll(v, 1, 1) for v in opaque]
            sooner = [pltpu.roll(v, LANES - 1, 1) for v in opaque] + [zero]
            for t in range(tiles + 1):
                right = jnp.where(lanes == LANES - 1, sooner[t + 1], sooner[t])
                ahead = ahead_ref[:, tile(t)]
                through = 1.0 - ahead
                front_ref[z, :, tile(t)] = g * through
                ahead_ref[:, tile(t)] = ahead + through * (right + g * (opaque[t] - right))
                if t:
                    left = jnp.where(lanes == 0, later[t - 1], later[t])
                    alpha = alpha_ref[:, tile(t)]
                    through = 1.0 - alpha
                    back_ref[z, :, tile(t)] = through - g * through
                    alpha_ref[:, tile(t)] = alpha + through * (opaque[t] + g * (left - opaque[t]))
                else:
                    back_ref[z, :, tile(t)] = zero
        return carry

    lax.fori_loop(0, depth // UNROLL, advance, 0)


def shade_kernel(shear_ref, sample_ref, front_ref, back_ref, alpha_ref, across_ref, deep_ref, down_ref,
                 slice_a_ref, slice_b_ref, row_a_ref, row_b_ref,
                 out_ref, shade_ref, moved_ref, above_ref, below_ref, now_ref, late_ref, *, depth_total, place, across):
    depth, rows, columns = across_ref.shape
    tiles = columns // LANES
    lanes = lane_ids()
    rows8 = row_ids()
    shear = shear_ref[0]
    start = place() * depth
    zero = jnp.zeros((8, LANES), jnp.float32)

    wide_odd = (place() & 1) == 1
    narrow_odd = (across() & 1) == 1
    row_a = row_a_ref[...].astype(jnp.float32)
    row_b = row_b_ref[...].astype(jnp.float32)
    above_ref[...] = -jnp.where(narrow_odd, row_a, row_b)
    below_ref[...] = jnp.where(narrow_odd, row_b, row_a)
    for z in range(depth):
        for t in range(LEFT):
            shade_ref[z, :, tile(t)] = zero
        for t in range(RIGHT):
            shade_ref[z, :, tile(LEFT + tiles + t)] = zero

    def shade(t, carry):
        here = pl.ds(pl.multiple_of(t * LANES, LANES), LANES)
        there = pl.ds(pl.multiple_of((t + LEFT) * LANES, LANES), LANES)
        for z in range(depth):
            above = jnp.broadcast_to(above_ref[z:z + 1, here], (8, LANES))
            below = jnp.broadcast_to(below_ref[z:z + 1, here], (8, LANES))
            extra = jnp.where(rows8 == 0, above, jnp.where(rows8 == 7, below, 0.0))
            down = down_ref[z, :, here] + extra
            deep = deep_ref[z, :, here]
            if z == 0 or z == depth - 1:
                slice_a = slice_a_ref[:, here].astype(jnp.float32)
                slice_b = slice_b_ref[:, here].astype(jnp.float32)
                if z == 0:
                    deep = deep - jnp.where(wide_odd, slice_a, slice_b)
                else:
                    deep = deep + jnp.where(wide_odd, slice_b, slice_a)
            side = across_ref[z, :, here]
            facing = 0.48 * side + 0.6 * down + 0.64 * deep
            strength = side * side + down * down + (deep * deep + 0.2)
            shade_ref[z, :, there] = 0.3 + 0.7 * facing * facing / strength
        return carry

    lax.fori_loop(0, tiles, shade, 0)

    def align(i, carry):
        for j in range(UNROLL):
            z = i * UNROLL + j
            whole, g = shift_of(shear, start + z, depth_total)
            hop, r = split_shift(whole)
            base = pl.multiple_of((1 - hop) * LANES, LANES)
            keep = lanes >= r
            rolled = [pltpu.roll(shade_ref[z, :, pl.ds(base + t * LANES, LANES)], r, 1) for t in range(tiles + 2)]
            for t in range(tiles + 1):
                moved_ref[z, :, tile(t)] = jnp.where(keep, rolled[t + 1], rolled[t])
        return carry

    lax.fori_loop(0, depth // UNROLL, align, 0)

    def gather(t, carry):
        here = pl.ds(pl.multiple_of(t * LANES, LANES), LANES)
        late = [zero] * 3
        now = [zero] * 3
        for z in range(depth):
            shading = moved_ref[z, :, here]
            front = front_ref[z, :, here] * shading
            back = back_ref[z, :, here] * shading
            for c in range(3):
                value = sample_ref[c, z, :, here]
                late[c] = late[c] + front * value
                now[c] = now[c] + back * value
        for c in range(3):
            late_ref[c, :, here] = late[c]
            now_ref[c, :, here] = now[c]
        return carry

    lax.fori_loop(0, tiles + 1, gather, 0)

    quarter = lax.shift_right_logical(lanes, 5)
    late = [[pltpu.roll(late_ref[c, :, tile(t)], 1, 1) for t in range(tiles + 1)] for c in range(3)]
    for t in range(tiles):
        parts = [now_ref[c, :, tile(t + 1)] + jnp.where(lanes == 0, late[c][t], late[c][t + 1]) for c in range(3)]
        parts = encode(parts, alpha_ref[:, tile(t + 1)], phase(place()))
        for y in range(4):
            moved = [parts[c] if c == y else pltpu.roll(parts[c], (32 * (c - y)) % LANES, 1) for c in range(4)]
            block = jnp.where(quarter < 2, jnp.where(quarter == 0, moved[0], moved[1]),
                              jnp.where(quarter == 2, moved[2], moved[3]))
            out_ref[(4 * t + y - TURN) % (4 * tiles)] = block.astype(jnp.int16)


def merge_kernel(shear_ref, parts_ref, out_ref):
    count = parts_ref.shape[0]
    lanes = lane_ids()
    flip = (shear_ref[0] & 1) == 1
    owner = 96 + (lanes & 31)
    total = jnp.zeros((8, LANES), jnp.float32)
    through = jnp.ones((8, LANES), jnp.float32)
    for i in range(count):
        slot = jnp.where(flip, count - 1 - i, i)
        alpha, value = decode(parts_ref[(slot - TURN) & (count - 1)], lanes, owner, phase(slot))
        total = total + through * value
        through = through - through * alpha
    for c in range(4):
        out_ref[c] = total[:, 32 * c:32 * c + 32]


def pairs(count, start):
    return [p for i in range(start, count - 1, 2) for p in ((i, i + 1), (i + 1, i))]


def per_device(density, color_table, opacity_table, view_shear, place=None, across=None, halos=None):
    depth, rows, columns = density.shape
    wide = 64
    depth_total = depth * wide
    if place is None:
        place = lambda: lax.axis_index("wide")
        across = lambda: lax.axis_index("narrow")
    f32 = jnp.float32
    vmem = pl.BlockSpec(memory_space=pltpu.VMEM)
    smem = pl.BlockSpec(memory_space=pltpu.SMEM)
    hbm = pl.BlockSpec(memory_space=pl.ANY)
    slab = (depth, rows, columns)
    wider = (depth, rows, columns + LANES)
    widest = (depth, rows, columns + (LEFT + RIGHT) * LANES)
    row = (rows, columns + LANES)
    density, color_table, opacity_table = [pltpu.with_memory_space_constraint(v, pltpu.HBM) for v in (density, color_table, opacity_table)]
    field, slice_a, slice_b, row_a, row_b = pl.pallas_call(
        functools.partial(prepare_kernel, place=place, across=across),
        in_specs=[hbm],
        out_specs=[vmem] * 5,
        out_shape=[pltpu.VMEM(widest, f32)] + [pltpu.VMEM((rows, columns), density.dtype)] * 2
        + [pltpu.VMEM((depth, columns), density.dtype)] * 2,
        scratch_shapes=[pltpu.VMEM(slab, density.dtype), pltpu.VMEM((depth, columns), f32),
                        pltpu.VMEM((depth, columns), f32), pltpu.SemaphoreType.DMA((CHUNKS,))],
        compiler_params=pltpu.CompilerParams(vmem_limit_bytes=LIMIT),
        name="prepare",
    )(density)
    if halos is None:
        row_a = lax.ppermute(row_a, "narrow", pairs(8, 0))
        row_b = lax.ppermute(row_b, "narrow", pairs(8, 1))
        slice_a = lax.ppermute(slice_a, "wide", pairs(wide, 0))
        slice_b = lax.ppermute(slice_b, "wide", pairs(wide, 1))
    else:
        slice_a, slice_b, row_a, row_b = halos
    local = pl.pallas_call(
        functools.partial(lookup_kernel, depth_total=depth_total, place=place),
        in_specs=[smem, vmem, hbm, hbm],
        out_specs=[vmem] * 7,
        out_shape=[pltpu.VMEM((3,) + wider, f32), pltpu.VMEM(wider, f32), pltpu.VMEM(wider, f32), pltpu.VMEM(row, f32),
                   pltpu.VMEM(slab, f32), pltpu.VMEM(slab, f32), pltpu.VMEM(slab, f32)],
        scratch_shapes=[pltpu.VMEM(wider, f32), pltpu.VMEM(wider, f32), pltpu.VMEM(row, f32),
                        pltpu.VMEM(color_table.shape, color_table.dtype),
                        pltpu.VMEM(opacity_table.shape, opacity_table.dtype), pltpu.SemaphoreType.DMA((2,))],
        compiler_params=pltpu.CompilerParams(vmem_limit_bytes=LIMIT),
        cost_estimate=pl.CostEstimate(flops=30_000_000, bytes_accessed=10_000_000, transcendentals=0),
        name="lookup",
    )(view_shear, field, color_table, opacity_table)
    bricks = pl.pallas_call(
        functools.partial(shade_kernel, depth_total=depth_total, place=place, across=across),
        in_specs=[smem] + [vmem] * 11,
        out_specs=vmem,
        out_shape=pltpu.VMEM((wide, rows, LANES), jnp.int16),
        scratch_shapes=[pltpu.VMEM(widest, f32), pltpu.VMEM(wider, f32), pltpu.VMEM((depth, columns), f32),
                        pltpu.VMEM((depth, columns), f32), pltpu.VMEM((3,) + row, f32), pltpu.VMEM((3,) + row, f32)],
        compiler_params=pltpu.CompilerParams(vmem_limit_bytes=LIMIT),
        name="shade",
    )(view_shear, *local, slice_a, slice_b, row_a, row_b)
    if halos is not None:
        return bricks
    order = [(i + TURN) % wide for i in range(wide)]
    parts = lax.all_to_all(bricks, "wide", split_axis=0, concat_axis=0, axis_index_groups=[order], tiled=True)
    return pl.pallas_call(
        merge_kernel,
        in_specs=[smem, vmem],
        out_specs=vmem,
        out_shape=jax.ShapeDtypeStruct((4, rows, 32), f32),
        name="merge",
    )(view_shear, parts)


def solution(mesh):
    placed = (P("wide", "narrow", None), P(), P(), P())
    return jax.shard_map(
        per_device, mesh=mesh, in_specs=placed, out_specs=P(None, "narrow", "wide"), check_vma=False
    )
```

```python
import functools

import jax
import jax.numpy as jnp
from jax import lax
from jax.experimental import pallas as pl
from jax.experimental.pallas import tpu as pltpu
from jax.sharding import Mesh, PartitionSpec as P

LANES = 128
LEFT = 3
RIGHT = 2
STEPS = 16
FEW = 4
OUTSIDE = -1.0 / 512
RATIO_STEPS = 65000.0
LOG_SPAN = 26.0
LOG_STEPS = 65534.0 / (LOG_SPAN - 1.85)
TINY = 1e-12
TURN = 36
CHUNKS = 4
LIMIT = 12 * 1024 * 1024


def lane_ids():
    return lax.broadcasted_iota(jnp.int32, (8, LANES), 1)


def row_ids():
    return lax.broadcasted_iota(jnp.int32, (8, LANES), 0)


def pick(table, index):
    return jnp.take_along_axis(table, index, axis=1, mode="promise_in_bounds")


def tile(t):
    return pl.ds(t * LANES, LANES)


def shift_of(shear, z, depth_total):
    numerator = shear * (2 * z + 1 - depth_total)
    denominator = 2 * depth_total
    bits = denominator.bit_length() - 1
    whole = lax.shift_right_arithmetic(numerator, bits)
    rest = numerator - lax.shift_left(whole, bits)
    return whole, rest.astype(jnp.float32) * (1.0 / denominator)


def split_shift(whole):
    hop = lax.shift_right_arithmetic(whole, 7)
    return hop, whole & 127


def next_lane(left, here, lanes):
    return jnp.where(lanes == 0, pltpu.roll(left, 1, 1), pltpu.roll(here, 1, 1))


def phase(place):
    return ((place * 39) & 63) * (1.0 / 64.0) if isinstance(place, int) else ((place * 39) & 63).astype(jnp.float32) * (1.0 / 64.0)


def encode(colors, alpha, offset):
    inverse = RATIO_STEPS / jnp.maximum(alpha, TINY)
    parts = [jnp.minimum(c * inverse + 0.5, 65535.0) for c in colors]
    level = jnp.log2(jnp.maximum(alpha, TINY)) * LOG_STEPS + (LOG_SPAN * LOG_STEPS + offset)
    parts.append(jnp.clip(level, 0.0, 65535.0))
    return [p.astype(jnp.int32) - 32768 for p in parts]


def decode(codes, lanes, owner, offset):
    value = codes.astype(jnp.int32).astype(jnp.float32) + 32768.0
    level = pick(value, owner)
    alpha = jnp.exp2((level + (0.5 - offset)) * (1.0 / LOG_STEPS) - LOG_SPAN)
    alpha = jnp.where(level > 0.0, alpha, 0.0)
    return alpha, alpha * jnp.where(lanes < 96, value * (1.0 / RATIO_STEPS), 1.0)


def prepare_kernel(dens_hbm, color_hbm, opacity_hbm,
                   field_ref, slice_a_ref, slice_b_ref, row_a_ref, row_b_ref, pair_ref, mixed_ref,
                   dens_ref, top_ref, bottom_ref, color_ref, opacity_ref, arrived, *, place, across):
    depth, rows, columns = dens_ref.shape
    tiles = columns // LANES
    chunk = depth // CHUNKS
    copies = [pltpu.make_async_copy(dens_hbm.at[pl.ds(i * chunk, chunk)], dens_ref.at[pl.ds(i * chunk, chunk)],
                                    arrived.at[i]) for i in range(CHUNKS)]
    tables = [pltpu.make_async_copy(color_hbm, color_ref, arrived.at[CHUNKS]),
              pltpu.make_async_copy(opacity_hbm, opacity_ref, arrived.at[CHUNKS + 1])]
    for copy in copies + tables:
        copy.start()
    outside = jnp.full((8, LANES), OUTSIDE, jnp.float32)
    for z in range(depth):
        for t in range(LEFT):
            field_ref[z, :, tile(t)] = outside
        for t in range(RIGHT):
            field_ref[z, :, tile(LEFT + tiles + t)] = outside
    for copy in tables:
        copy.wait()
    lanes = lane_ids()
    half = (2 * lanes) & 127
    low = lanes < 64
    rows_of = [color_ref[c:c + 1, :] for c in range(3)] + [opacity_ref[...].reshape(1, -1)]
    for i in range(2):
        red, green, blue, opacity = [
            jnp.where(low, pick(jnp.broadcast_to(row[:, :LANES], (8, LANES)), half + i),
                      pick(jnp.broadcast_to(row[:, LANES:], (8, LANES)), half + i))
            for row in [r.astype(jnp.float32) for r in rows_of]]
        pair_ref[i] = (jnp.floor(red * 32767.0 + 0.5).astype(jnp.int32) * 65536
                       + jnp.floor(green * 65535.0 + 0.5).astype(jnp.int32))
        mixed_ref[i] = opacity + opacity * (blue * (1.0 / 512.0))
    for i in range(CHUNKS):
        copies[i].wait()
        for z in range(i * chunk, (i + 1) * chunk):
            slab = dens_ref[z].astype(jnp.float32)
            field_ref[z, :, pl.ds(LEFT * LANES, columns)] = slab
            top_ref[z:z + 1, :] = slab[:1]
            bottom_ref[z:z + 1, :] = slab[rows - 1:]
    wide_odd = (place() & 1) == 1
    narrow_odd = (across() & 1) == 1
    top, bottom = top_ref[...], bottom_ref[...]
    row_a_ref[...] = jnp.where(narrow_odd, top, bottom).astype(jnp.bfloat16)
    row_b_ref[...] = jnp.where(narrow_odd, bottom, top).astype(jnp.bfloat16)
    first = field_ref[0, :, pl.ds(LEFT * LANES, columns)]
    last = field_ref[depth - 1, :, pl.ds(LEFT * LANES, columns)]
    slice_a_ref[...] = jnp.where(wide_odd, first, last).astype(jnp.bfloat16)
    slice_b_ref[...] = jnp.where(wide_odd, last, first).astype(jnp.bfloat16)


def lookup_kernel(shear_ref, field_ref, pair_ref, mixed_ref,
                  sample_ref, front_ref, back_ref, alpha_ref, across_ref, deep_ref, down_ref,
                  opaque_ref, ahead_ref, *, depth_total, place):
    depth, rows, columns = across_ref.shape
    tiles = columns // LANES
    lanes = lane_ids()
    rows8 = row_ids()
    shear = shear_ref[0]
    start = place() * depth
    flip = (shear & 1) == 1
    zero = jnp.zeros((8, LANES), jnp.float32)
    def slopes(z):
        if True:
            before = lax.max(z - 1, 0)
            after = lax.min(z + 1, depth - 1)
            inner_low = jnp.where(z > 0, 1.0, 0.0)
            inner_high = jnp.where(z < depth - 1, 1.0, 0.0)
            slabs = [field_ref[z, :, tile(LEFT + t)] for t in range(tiles)]
            later = [zero] + [pltpu.roll(v, 1, 1) for v in slabs]
            sooner = [pltpu.roll(v, LANES - 1, 1) for v in slabs] + [zero]
            for t in range(tiles):
                left = jnp.where(lanes == 0, later[t], later[t + 1])
                right = jnp.where(lanes == LANES - 1, sooner[t + 1], sooner[t])
                below = jnp.where(rows8 == 7, 0.0, pltpu.roll(slabs[t], 7, 0))
                above = jnp.where(rows8 == 0, 0.0, pltpu.roll(slabs[t], 1, 0))
                across_ref[z, :, tile(t)] = right - left
                down_ref[z, :, tile(t)] = below - above
                deep_ref[z, :, tile(t)] = (inner_high * field_ref[after, :, tile(LEFT + t)]
                                           - inner_low * field_ref[before, :, tile(LEFT + t)])

    evens, odds = [[pair_ref[i], mixed_ref[i]] for i in range(2)]

    def split(word):
        return [lax.shift_right_logical(word, 16).astype(jnp.float32), (word & 65535).astype(jnp.float32)]

    def part(word):
        wide = word * 65537.0
        opacity = wide - (wide - word)
        return [(word - opacity) * pltpu.reciprocal(opacity, approx=True), opacity]

    def sample(i, carry):
        for j in range(FEW):
            slopes(i * FEW + j)
        values = {}
        for j in range(FEW):
            z = i * FEW + j
            whole, g = shift_of(shear, start + z, depth_total)
            hop, r = split_shift(whole)
            base = pl.multiple_of((1 - hop) * LANES, LANES)
            keep = lanes >= r
            rolled = [pltpu.roll(field_ref[z, :, pl.ds(base + t * LANES, LANES)], r, 1) for t in range(tiles + 2)]
            for t in range(tiles + 1):
                values[j, t] = jnp.where(keep, rolled[t + 1], rolled[t])
        for j, t in [(j, t) for j in range(FEW) for t in range(tiles + 1)]:
            z = i * FEW + j
            value = values[j, t]
            scaled = value * 255.0
            level = jnp.minimum(scaled.astype(jnp.int32), 254)
            even = lax.shift_right_logical(level + 1, 1)
            odd = lax.shift_right_logical(level, 1)
            weight = jnp.abs(scaled - (2 * even).astype(jnp.float32))
            lower = [pick(table, even) for table in evens]
            upper = [pick(table, odd) for table in odds]
            lower = split(lower[0]) + part(lower[1])
            upper = split(upper[0]) + part(upper[1])
            mixed = [e + weight * (o - e) for e, o in zip(lower, upper)]
            opacity = jnp.where(value >= 0.0, mixed[3], 0.0)
            sample_ref[0, z, :, tile(t)] = mixed[0] * (opacity * (1.0 / 32767.0))
            sample_ref[1, z, :, tile(t)] = mixed[1] * (opacity * (1.0 / 65535.0))
            sample_ref[2, z, :, tile(t)] = mixed[2] * (opacity * 512.0)
            opaque_ref[z, :, tile(t)] = opacity
        return carry

    lax.fori_loop(0, depth // FEW, sample, 0)

    for t in range(tiles + 1):
        alpha_ref[:, tile(t)] = zero
        ahead_ref[:, tile(t)] = zero

    def advance(i, carry):
        places, parts = [], []
        for j in range(STEPS):
            step = i * STEPS + j
            places.append(jnp.where(flip, depth - 1 - step, step))
            parts.append(shift_of(shear, start + places[j], depth_total)[1])
        here = [opaque_ref[z, :, tile(0)] for z in places]
        later = [None] * STEPS
        sooner = [pltpu.roll(v, LANES - 1, 1) for v in here]
        for t in range(tiles + 1):
            ahead = ahead_ref[:, tile(t)]
            alpha = alpha_ref[:, tile(t)]
            for j in range(STEPS):
                z, g, opaque = places[j], parts[j], here[j]
                if t < tiles:
                    here[j] = opaque_ref[z, :, tile(t + 1)]
                    follow = pltpu.roll(here[j], LANES - 1, 1)
                    right = jnp.where(lanes == LANES - 1, follow, sooner[j])
                    sooner[j] = follow
                else:
                    right = sooner[j]
                through = 1.0 - ahead
                front_ref[z, :, tile(t)] = g * through
                ahead = ahead + through * (right + g * (opaque - right))
                behind = pltpu.roll(opaque, 1, 1)
                if t:
                    left = jnp.where(lanes == 0, later[j], behind)
                    through = 1.0 - alpha
                    back_ref[z, :, tile(t)] = through - g * through
                    alpha = alpha + through * (opaque + g * (left - opaque))
                else:
                    back_ref[z, :, tile(t)] = zero
                later[j] = behind
            ahead_ref[:, tile(t)] = ahead
            alpha_ref[:, tile(t)] = alpha
        return carry

    lax.fori_loop(0, depth // STEPS, advance, 0)


def shade_kernel(shear_ref, sample_ref, front_ref, back_ref, alpha_ref, across_ref, deep_ref, down_ref,
                 slice_a_ref, slice_b_ref, row_a_ref, row_b_ref,
                 out_ref, shade_ref, moved_ref, above_ref, below_ref, now_ref, late_ref, *, depth_total, place, across):
    depth, rows, columns = across_ref.shape
    tiles = columns // LANES
    lanes = lane_ids()
    rows8 = row_ids()
    shear = shear_ref[0]
    start = place() * depth
    zero = jnp.zeros((8, LANES), jnp.float32)

    wide_odd = (place() & 1) == 1
    narrow_odd = (across() & 1) == 1
    row_a = row_a_ref[...].astype(jnp.float32)
    row_b = row_b_ref[...].astype(jnp.float32)
    above_ref[...] = -jnp.where(narrow_odd, row_a, row_b)
    below_ref[...] = jnp.where(narrow_odd, row_b, row_a)
    for z in range(depth):
        for t in range(LEFT):
            shade_ref[z, :, tile(t)] = zero
        for t in range(RIGHT):
            shade_ref[z, :, tile(LEFT + tiles + t)] = zero

    def shade(t, carry):
        here = pl.ds(pl.multiple_of(t * LANES, LANES), LANES)
        there = pl.ds(pl.multiple_of((t + LEFT) * LANES, LANES), LANES)
        for z in range(depth):
            above = jnp.broadcast_to(above_ref[z:z + 1, here], (8, LANES))
            below = jnp.broadcast_to(below_ref[z:z + 1, here], (8, LANES))
            extra = jnp.where(rows8 == 0, above, jnp.where(rows8 == 7, below, 0.0))
            down = down_ref[z, :, here] + extra
            deep = deep_ref[z, :, here]
            if z == 0 or z == depth - 1:
                slice_a = slice_a_ref[:, here].astype(jnp.float32)
                slice_b = slice_b_ref[:, here].astype(jnp.float32)
                if z == 0:
                    deep = deep - jnp.where(wide_odd, slice_a, slice_b)
                else:
                    deep = deep + jnp.where(wide_odd, slice_b, slice_a)
            side = across_ref[z, :, here]
            facing = 0.48 * side + 0.6 * down + 0.64 * deep
            strength = side * side + down * down + (deep * deep + 0.2)
            shade_ref[z, :, there] = 0.3 + 0.7 * facing * facing / strength
        return carry

    lax.fori_loop(0, tiles, shade, 0)

    def align(i, carry):
        for j in range(STEPS):
            z = i * STEPS + j
            whole, g = shift_of(shear, start + z, depth_total)
            hop, r = split_shift(whole)
            base = pl.multiple_of((1 - hop) * LANES, LANES)
            keep = lanes >= r
            rolled = [pltpu.roll(shade_ref[z, :, pl.ds(base + t * LANES, LANES)], r, 1) for t in range(tiles + 2)]
            for t in range(tiles + 1):
                moved_ref[z, :, tile(t)] = jnp.where(keep, rolled[t + 1], rolled[t])
        return carry

    lax.fori_loop(0, depth // STEPS, align, 0)

    def gather(t, carry):
        here = pl.ds(pl.multiple_of(t * LANES, LANES), LANES)
        late = [zero] * 3
        now = [zero] * 3
        for z in range(depth):
            shading = moved_ref[z, :, here]
            front = front_ref[z, :, here] * shading
            back = back_ref[z, :, here] * shading
            for c in range(3):
                value = sample_ref[c, z, :, here]
                late[c] = late[c] + front * value
                now[c] = now[c] + back * value
        for c in range(3):
            late_ref[c, :, here] = late[c]
            now_ref[c, :, here] = now[c]
        return carry

    lax.fori_loop(0, tiles + 1, gather, 0)

    quarter = lax.shift_right_logical(lanes, 5)
    late = [[pltpu.roll(late_ref[c, :, tile(t)], 1, 1) for t in range(tiles + 1)] for c in range(3)]
    for t in range(tiles):
        parts = [now_ref[c, :, tile(t + 1)] + jnp.where(lanes == 0, late[c][t], late[c][t + 1]) for c in range(3)]
        parts = encode(parts, alpha_ref[:, tile(t + 1)], phase(place()))
        for y in range(4):
            moved = [parts[c] if c == y else pltpu.roll(parts[c], (32 * (c - y)) % LANES, 1) for c in range(4)]
            block = jnp.where(quarter < 2, jnp.where(quarter == 0, moved[0], moved[1]),
                              jnp.where(quarter == 2, moved[2], moved[3]))
            out_ref[(4 * t + y - TURN) % (4 * tiles)] = block.astype(jnp.int16)


def merge_kernel(shear_ref, parts_ref, out_ref):
    count = parts_ref.shape[0]
    lanes = lane_ids()
    flip = (shear_ref[0] & 1) == 1
    owner = 96 + (lanes & 31)
    total = jnp.zeros((8, LANES), jnp.float32)
    through = jnp.ones((8, LANES), jnp.float32)
    for i in range(count):
        slot = jnp.where(flip, count - 1 - i, i)
        alpha, value = decode(parts_ref[(slot - TURN) & (count - 1)], lanes, owner, phase(slot))
        total = total + through * value
        through = through - through * alpha
    for c in range(4):
        out_ref[c] = total[:, 32 * c:32 * c + 32]


def pairs(count, start):
    return [p for i in range(start, count - 1, 2) for p in ((i, i + 1), (i + 1, i))]


def per_device(density, color_table, opacity_table, view_shear, place=None, across=None, halos=None):
    depth, rows, columns = density.shape
    wide = 64
    depth_total = depth * wide
    if place is None:
        place = lambda: lax.axis_index("wide")
        across = lambda: lax.axis_index("narrow")
    f32 = jnp.float32
    vmem = pl.BlockSpec(memory_space=pltpu.VMEM)
    smem = pl.BlockSpec(memory_space=pltpu.SMEM)
    hbm = pl.BlockSpec(memory_space=pl.ANY)
    slab = (depth, rows, columns)
    wider = (depth, rows, columns + LANES)
    widest = (depth, rows, columns + (LEFT + RIGHT) * LANES)
    row = (rows, columns + LANES)
    density, color_table, opacity_table = [pltpu.with_memory_space_constraint(v, pltpu.HBM) for v in (density, color_table, opacity_table)]
    field, slice_a, slice_b, row_a, row_b, pair, mixed = pl.pallas_call(
        functools.partial(prepare_kernel, place=place, across=across),
        in_specs=[hbm] * 3,
        out_specs=[vmem] * 7,
        out_shape=[pltpu.VMEM(widest, f32)] + [pltpu.VMEM((rows, columns), density.dtype)] * 2
        + [pltpu.VMEM((depth, columns), density.dtype)] * 2
        + [pltpu.VMEM((2, rows, LANES), jnp.int32), pltpu.VMEM((2, rows, LANES), f32)],
        scratch_shapes=[pltpu.VMEM(slab, density.dtype), pltpu.VMEM((depth, columns), f32),
                        pltpu.VMEM((depth, columns), f32), pltpu.VMEM(color_table.shape, color_table.dtype),
                        pltpu.VMEM(opacity_table.shape, opacity_table.dtype), pltpu.SemaphoreType.DMA((CHUNKS + 2,))],
        compiler_params=pltpu.CompilerParams(vmem_limit_bytes=LIMIT),
        name="prepare",
    )(density, color_table, opacity_table)
    if halos is None:
        row_a = lax.ppermute(row_a, "narrow", pairs(8, 0))
        row_b = lax.ppermute(row_b, "narrow", pairs(8, 1))
        slice_a = lax.ppermute(slice_a, "wide", pairs(wide, 0))
        slice_b = lax.ppermute(slice_b, "wide", pairs(wide, 1))
    else:
        slice_a, slice_b, row_a, row_b = halos
    local = pl.pallas_call(
        functools.partial(lookup_kernel, depth_total=depth_total, place=place),
        in_specs=[smem, vmem, vmem, vmem],
        out_specs=[vmem] * 7,
        out_shape=[pltpu.VMEM((3,) + wider, f32), pltpu.VMEM(wider, f32), pltpu.VMEM(wider, f32), pltpu.VMEM(row, f32),
                   pltpu.VMEM(slab, f32), pltpu.VMEM(slab, f32), pltpu.VMEM(slab, f32)],
        scratch_shapes=[pltpu.VMEM(wider, f32), pltpu.VMEM(row, f32)],
        compiler_params=pltpu.CompilerParams(vmem_limit_bytes=LIMIT),
        cost_estimate=pl.CostEstimate(flops=30_000_000, bytes_accessed=10_000_000, transcendentals=0),
        name="lookup",
    )(view_shear, field, pair, mixed)
    bricks = pl.pallas_call(
        functools.partial(shade_kernel, depth_total=depth_total, place=place, across=across),
        in_specs=[smem] + [vmem] * 11,
        out_specs=vmem,
        out_shape=pltpu.VMEM((wide, rows, LANES), jnp.int16),
        scratch_shapes=[pltpu.VMEM(widest, f32), pltpu.VMEM(wider, f32), pltpu.VMEM((depth, columns), f32),
                        pltpu.VMEM((depth, columns), f32), pltpu.VMEM((3,) + row, f32), pltpu.VMEM((3,) + row, f32)],
        compiler_params=pltpu.CompilerParams(vmem_limit_bytes=LIMIT),
        name="shade",
    )(view_shear, *local, slice_a, slice_b, row_a, row_b)
    if halos is not None:
        return bricks
    order = [(i + TURN) % wide for i in range(wide)]
    parts = lax.all_to_all(bricks, "wide", split_axis=0, concat_axis=0, axis_index_groups=[order], tiled=True)
    return pl.pallas_call(
        merge_kernel,
        in_specs=[smem, vmem],
        out_specs=vmem,
        out_shape=jax.ShapeDtypeStruct((4, rows, 32), f32),
        name="merge",
    )(view_shear, parts)


def solution(mesh):
    placed = (P("wide", "narrow", None), P(), P(), P())
    return jax.shard_map(
        per_device, mesh=mesh, in_specs=placed, out_specs=P(None, "narrow", "wide"), check_vma=False
    )
```

```python
import functools

import jax
import jax.numpy as jnp
from jax import lax
from jax.experimental import pallas as pl
from jax.experimental.pallas import tpu as pltpu
from jax.sharding import Mesh, PartitionSpec as P

LANES = 128
LEFT = 3
RIGHT = 2
STEPS = 16
FEW = 4
OUTSIDE = -1.0 / 512
RATIO_STEPS = 65000.0
LOG_SPAN = 26.0
LOG_STEPS = 65534.0 / (LOG_SPAN - 1.85)
TINY = 1e-12
TURN = 36
CHUNKS = 2
LIMIT = 12 * 1024 * 1024


def lane_ids():
    return lax.broadcasted_iota(jnp.int32, (8, LANES), 1)


def row_ids():
    return lax.broadcasted_iota(jnp.int32, (8, LANES), 0)


def pick(table, index):
    return jnp.take_along_axis(table, index, axis=1, mode="promise_in_bounds")


def tile(t):
    return pl.ds(t * LANES, LANES)


def shift_of(shear, z, depth_total):
    numerator = shear * (2 * z + 1 - depth_total)
    denominator = 2 * depth_total
    bits = denominator.bit_length() - 1
    whole = lax.shift_right_arithmetic(numerator, bits)
    rest = numerator - lax.shift_left(whole, bits)
    return whole, rest.astype(jnp.float32) * (1.0 / denominator)


def split_shift(whole):
    hop = lax.shift_right_arithmetic(whole, 7)
    return hop, whole & 127


def next_lane(left, here, lanes):
    return jnp.where(lanes == 0, pltpu.roll(left, 1, 1), pltpu.roll(here, 1, 1))


def phase(place):
    return ((place * 39) & 63) * (1.0 / 64.0) if isinstance(place, int) else ((place * 39) & 63).astype(jnp.float32) * (1.0 / 64.0)


def encode(colors, alpha, offset):
    inverse = RATIO_STEPS / jnp.maximum(alpha, TINY)
    parts = [jnp.minimum(c * inverse + 0.5, 65535.0) for c in colors]
    level = jnp.log2(jnp.maximum(alpha, TINY)) * LOG_STEPS + (LOG_SPAN * LOG_STEPS + offset)
    parts.append(jnp.clip(level, 0.0, 65535.0))
    return [p.astype(jnp.int32) - 32768 for p in parts]


def decode(codes, lanes, owner, offset):
    value = codes.astype(jnp.int32).astype(jnp.float32) + 32768.0
    level = pick(value, owner)
    alpha = jnp.exp2((level + (0.5 - offset)) * (1.0 / LOG_STEPS) - LOG_SPAN)
    alpha = jnp.where(level > 0.0, alpha, 0.0)
    return alpha, alpha * jnp.where(lanes < 96, value * (1.0 / RATIO_STEPS), 1.0)


def prepare_kernel(dens_hbm, color_hbm, opacity_hbm,
                   field_ref, slice_a_ref, slice_b_ref, row_a_ref, row_b_ref, pair_ref, mixed_ref,
                   dens_ref, top_ref, bottom_ref, color_ref, opacity_ref, arrived, *, place, across):
    depth, rows, columns = dens_ref.shape
    tiles = columns // LANES
    chunk = depth // CHUNKS
    copies = [pltpu.make_async_copy(dens_hbm.at[pl.ds(i * chunk, chunk)], dens_ref.at[pl.ds(i * chunk, chunk)],
                                    arrived.at[i]) for i in range(CHUNKS)]
    tables = [pltpu.make_async_copy(color_hbm, color_ref, arrived.at[CHUNKS]),
              pltpu.make_async_copy(opacity_hbm, opacity_ref, arrived.at[CHUNKS + 1])]
    for copy in copies + tables:
        copy.start()
    outside = jnp.full((8, LANES), OUTSIDE, jnp.float32)
    for z in range(depth):
        for t in range(LEFT):
            field_ref[z, :, tile(t)] = outside
        for t in range(RIGHT):
            field_ref[z, :, tile(LEFT + tiles + t)] = outside
    for copy in tables:
        copy.wait()
    lanes = lane_ids()
    half = (2 * lanes) & 127
    low = lanes < 64
    rows_of = [color_ref[c:c + 1, :] for c in range(3)] + [opacity_ref[...].reshape(1, -1)]
    for i in range(2):
        red, green, blue, opacity = [
            jnp.where(low, pick(jnp.broadcast_to(row[:, :LANES], (8, LANES)), half + i),
                      pick(jnp.broadcast_to(row[:, LANES:], (8, LANES)), half + i))
            for row in [r.astype(jnp.float32) for r in rows_of]]
        pair_ref[i] = (jnp.floor(red * 32767.0 + 0.5).astype(jnp.int32) * 65536
                       + jnp.floor(green * 65535.0 + 0.5).astype(jnp.int32))
        mixed_ref[i] = opacity + opacity * (blue * (1.0 / 512.0))
    for i in range(CHUNKS):
        copies[i].wait()
        for z in range(i * chunk, (i + 1) * chunk):
            slab = dens_ref[z].astype(jnp.float32)
            field_ref[z, :, pl.ds(LEFT * LANES, columns)] = slab
            top_ref[z:z + 1, :] = slab[:1]
            bottom_ref[z:z + 1, :] = slab[rows - 1:]
    wide_odd = (place() & 1) == 1
    narrow_odd = (across() & 1) == 1
    top, bottom = top_ref[...], bottom_ref[...]
    row_a_ref[...] = jnp.where(narrow_odd, top, bottom).astype(jnp.bfloat16)
    row_b_ref[...] = jnp.where(narrow_odd, bottom, top).astype(jnp.bfloat16)
    first = field_ref[0, :, pl.ds(LEFT * LANES, columns)]
    last = field_ref[depth - 1, :, pl.ds(LEFT * LANES, columns)]
    slice_a_ref[...] = jnp.where(wide_odd, first, last).astype(jnp.bfloat16)
    slice_b_ref[...] = jnp.where(wide_odd, last, first).astype(jnp.bfloat16)


def lookup_kernel(shear_ref, field_ref, pair_ref, mixed_ref,
                  sample_ref, front_ref, back_ref, alpha_ref, across_ref, deep_ref, down_ref,
                  opaque_ref, ahead_ref, *, depth_total, place):
    depth, rows, columns = across_ref.shape
    tiles = columns // LANES
    lanes = lane_ids()
    rows8 = row_ids()
    shear = shear_ref[0]
    start = place() * depth
    flip = (shear & 1) == 1
    zero = jnp.zeros((8, LANES), jnp.float32)
    def slopes(z):
        if True:
            before = lax.max(z - 1, 0)
            after = lax.min(z + 1, depth - 1)
            inner_low = jnp.where(z > 0, 1.0, 0.0)
            inner_high = jnp.where(z < depth - 1, 1.0, 0.0)
            slabs = [field_ref[z, :, tile(LEFT + t)] for t in range(tiles)]
            later = [zero] + [pltpu.roll(v, 1, 1) for v in slabs]
            sooner = [pltpu.roll(v, LANES - 1, 1) for v in slabs] + [zero]
            for t in range(tiles):
                left = jnp.where(lanes == 0, later[t], later[t + 1])
                right = jnp.where(lanes == LANES - 1, sooner[t + 1], sooner[t])
                below = jnp.where(rows8 == 7, 0.0, pltpu.roll(slabs[t], 7, 0))
                above = jnp.where(rows8 == 0, 0.0, pltpu.roll(slabs[t], 1, 0))
                across_ref[z, :, tile(t)] = right - left
                down_ref[z, :, tile(t)] = below - above
                deep_ref[z, :, tile(t)] = (inner_high * field_ref[after, :, tile(LEFT + t)]
                                           - inner_low * field_ref[before, :, tile(LEFT + t)])

    evens, odds = [[pair_ref[i], mixed_ref[i]] for i in range(2)]

    def split(word):
        return [lax.shift_right_logical(word, 16).astype(jnp.float32), (word & 65535).astype(jnp.float32)]

    def part(word):
        wide = word * 65537.0
        opacity = wide - (wide - word)
        return [(word - opacity) * pltpu.reciprocal(opacity, approx=True), opacity]

    def sample(i, carry):
        for j in range(FEW):
            slopes(i * FEW + j)
        values = {}
        for j in range(FEW):
            z = i * FEW + j
            whole, g = shift_of(shear, start + z, depth_total)
            hop, r = split_shift(whole)
            base = pl.multiple_of((1 - hop) * LANES, LANES)
            keep = lanes >= r
            rolled = [pltpu.roll(field_ref[z, :, pl.ds(base + t * LANES, LANES)], r, 1) for t in range(tiles + 2)]
            for t in range(tiles + 1):
                values[j, t] = jnp.where(keep, rolled[t + 1], rolled[t])
        for j, t in [(j, t) for j in range(FEW) for t in range(tiles + 1)]:
            z = i * FEW + j
            value = values[j, t]
            scaled = value * 255.0
            level = jnp.minimum(scaled.astype(jnp.int32), 254)
            even = lax.shift_right_logical(level + 1, 1)
            odd = lax.shift_right_logical(level, 1)
            weight = jnp.abs(scaled - (2 * even).astype(jnp.float32))
            lower = [pick(table, even) for table in evens]
            upper = [pick(table, odd) for table in odds]
            lower = split(lower[0]) + part(lower[1])
            upper = split(upper[0]) + part(upper[1])
            mixed = [e + weight * (o - e) for e, o in zip(lower, upper)]
            opacity = jnp.where(value >= 0.0, mixed[3], 0.0)
            sample_ref[0, z, :, tile(t)] = mixed[0] * (opacity * (1.0 / 32767.0))
            sample_ref[1, z, :, tile(t)] = mixed[1] * (opacity * (1.0 / 65535.0))
            sample_ref[2, z, :, tile(t)] = mixed[2] * (opacity * 512.0)
            opaque_ref[z, :, tile(t)] = opacity
        return carry

    lax.fori_loop(0, depth // FEW, sample, 0)

    for t in range(tiles + 1):
        alpha_ref[:, tile(t)] = zero
        ahead_ref[:, tile(t)] = zero

    def advance(i, carry):
        places, parts = [], []
        for j in range(STEPS):
            step = i * STEPS + j
            places.append(jnp.where(flip, depth - 1 - step, step))
            parts.append(shift_of(shear, start + places[j], depth_total)[1])
        here = [opaque_ref[z, :, tile(0)] for z in places]
        later = [None] * STEPS
        sooner = [pltpu.roll(v, LANES - 1, 1) for v in here]
        for t in range(tiles + 1):
            ahead = ahead_ref[:, tile(t)]
            alpha = alpha_ref[:, tile(t)]
            for j in range(STEPS):
                z, g, opaque = places[j], parts[j], here[j]
                if t < tiles:
                    here[j] = opaque_ref[z, :, tile(t + 1)]
                    follow = pltpu.roll(here[j], LANES - 1, 1)
                    right = jnp.where(lanes == LANES - 1, follow, sooner[j])
                    sooner[j] = follow
                else:
                    right = sooner[j]
                through = 1.0 - ahead
                front_ref[z, :, tile(t)] = g * through
                ahead = ahead + through * (right + g * (opaque - right))
                behind = pltpu.roll(opaque, 1, 1)
                if t:
                    left = jnp.where(lanes == 0, later[j], behind)
                    through = 1.0 - alpha
                    back_ref[z, :, tile(t)] = through - g * through
                    alpha = alpha + through * (opaque + g * (left - opaque))
                else:
                    back_ref[z, :, tile(t)] = zero
                later[j] = behind
            ahead_ref[:, tile(t)] = ahead
            alpha_ref[:, tile(t)] = alpha
        return carry

    lax.fori_loop(0, depth // STEPS, advance, 0)


def shade_kernel(shear_ref, sample_ref, front_ref, back_ref, alpha_ref, across_ref, deep_ref, down_ref,
                 slice_a_ref, slice_b_ref, row_a_ref, row_b_ref,
                 out_ref, shade_ref, moved_ref, above_ref, below_ref, now_ref, late_ref, *, depth_total, place, across):
    depth, rows, columns = across_ref.shape
    tiles = columns // LANES
    lanes = lane_ids()
    rows8 = row_ids()
    shear = shear_ref[0]
    start = place() * depth
    zero = jnp.zeros((8, LANES), jnp.float32)

    wide_odd = (place() & 1) == 1
    narrow_odd = (across() & 1) == 1
    row_a = row_a_ref[...].astype(jnp.float32)
    row_b = row_b_ref[...].astype(jnp.float32)
    above_ref[...] = -jnp.where(narrow_odd, row_a, row_b)
    below_ref[...] = jnp.where(narrow_odd, row_b, row_a)
    for z in range(depth):
        for t in range(LEFT):
            shade_ref[z, :, tile(t)] = zero
        for t in range(RIGHT):
            shade_ref[z, :, tile(LEFT + tiles + t)] = zero

    def shade(t, carry):
        here = pl.ds(pl.multiple_of(t * LANES, LANES), LANES)
        there = pl.ds(pl.multiple_of((t + LEFT) * LANES, LANES), LANES)
        for z in range(depth):
            above = jnp.broadcast_to(above_ref[z:z + 1, here], (8, LANES))
            below = jnp.broadcast_to(below_ref[z:z + 1, here], (8, LANES))
            extra = jnp.where(rows8 == 0, above, jnp.where(rows8 == 7, below, 0.0))
            down = down_ref[z, :, here] + extra
            deep = deep_ref[z, :, here]
            if z == 0 or z == depth - 1:
                slice_a = slice_a_ref[:, here].astype(jnp.float32)
                slice_b = slice_b_ref[:, here].astype(jnp.float32)
                if z == 0:
                    deep = deep - jnp.where(wide_odd, slice_a, slice_b)
                else:
                    deep = deep + jnp.where(wide_odd, slice_b, slice_a)
            side = across_ref[z, :, here]
            facing = 0.48 * side + 0.6 * down + 0.64 * deep
            strength = side * side + down * down + (deep * deep + 0.2)
            shade_ref[z, :, there] = 0.3 + 0.7 * facing * facing / strength
        return carry

    lax.fori_loop(0, tiles, shade, 0)

    def align(i, carry):
        for j in range(STEPS):
            z = i * STEPS + j
            whole, g = shift_of(shear, start + z, depth_total)
            hop, r = split_shift(whole)
            base = pl.multiple_of((1 - hop) * LANES, LANES)
            keep = lanes >= r
            rolled = [pltpu.roll(shade_ref[z, :, pl.ds(base + t * LANES, LANES)], r, 1) for t in range(tiles + 2)]
            for t in range(tiles + 1):
                moved_ref[z, :, tile(t)] = jnp.where(keep, rolled[t + 1], rolled[t])
        return carry

    lax.fori_loop(0, depth // STEPS, align, 0)

    def gather(t, carry):
        here = pl.ds(pl.multiple_of(t * LANES, LANES), LANES)
        late = [zero] * 3
        now = [zero] * 3
        for z in range(depth):
            shading = moved_ref[z, :, here]
            front = front_ref[z, :, here] * shading
            back = back_ref[z, :, here] * shading
            for c in range(3):
                value = sample_ref[c, z, :, here]
                late[c] = late[c] + front * value
                now[c] = now[c] + back * value
        for c in range(3):
            late_ref[c, :, here] = late[c]
            now_ref[c, :, here] = now[c]
        return carry

    lax.fori_loop(0, tiles + 1, gather, 0)

    quarter = lax.shift_right_logical(lanes, 5)
    late = [[pltpu.roll(late_ref[c, :, tile(t)], 1, 1) for t in range(tiles + 1)] for c in range(3)]
    for t in range(tiles):
        parts = [now_ref[c, :, tile(t + 1)] + jnp.where(lanes == 0, late[c][t], late[c][t + 1]) for c in range(3)]
        parts = encode(parts, alpha_ref[:, tile(t + 1)], phase(place()))
        for y in range(4):
            moved = [parts[c] if c == y else pltpu.roll(parts[c], (32 * (c - y)) % LANES, 1) for c in range(4)]
            block = jnp.where(quarter < 2, jnp.where(quarter == 0, moved[0], moved[1]),
                              jnp.where(quarter == 2, moved[2], moved[3]))
            out_ref[(4 * t + y - TURN) % (4 * tiles)] = block.astype(jnp.int16)


def merge_kernel(shear_ref, parts_ref, out_ref):
    count = parts_ref.shape[0]
    lanes = lane_ids()
    flip = (shear_ref[0] & 1) == 1
    owner = 96 + (lanes & 31)
    total = jnp.zeros((8, LANES), jnp.float32)
    through = jnp.ones((8, LANES), jnp.float32)
    for i in range(count):
        slot = jnp.where(flip, count - 1 - i, i)
        alpha, value = decode(parts_ref[(slot - TURN) & (count - 1)], lanes, owner, phase(slot))
        total = total + through * value
        through = through - through * alpha
    for c in range(4):
        out_ref[c] = total[:, 32 * c:32 * c + 32]


def pairs(count, start):
    return [p for i in range(start, count - 1, 2) for p in ((i, i + 1), (i + 1, i))]


def per_device(density, color_table, opacity_table, view_shear, place=None, across=None, halos=None):
    depth, rows, columns = density.shape
    wide = 64
    depth_total = depth * wide
    if place is None:
        place = lambda: lax.axis_index("wide")
        across = lambda: lax.axis_index("narrow")
    f32 = jnp.float32
    vmem = pl.BlockSpec(memory_space=pltpu.VMEM)
    smem = pl.BlockSpec(memory_space=pltpu.SMEM)
    hbm = pl.BlockSpec(memory_space=pl.ANY)
    slab = (depth, rows, columns)
    wider = (depth, rows, columns + LANES)
    widest = (depth, rows, columns + (LEFT + RIGHT) * LANES)
    row = (rows, columns + LANES)
    density, color_table, opacity_table = [pltpu.with_memory_space_constraint(v, pltpu.HBM) for v in (density, color_table, opacity_table)]
    field, slice_a, slice_b, row_a, row_b, pair, mixed = pl.pallas_call(
        functools.partial(prepare_kernel, place=place, across=across),
        in_specs=[hbm] * 3,
        out_specs=[vmem] * 7,
        out_shape=[pltpu.VMEM(widest, f32)] + [pltpu.VMEM((rows, columns), density.dtype)] * 2
        + [pltpu.VMEM((depth, columns), density.dtype)] * 2
        + [pltpu.VMEM((2, rows, LANES), jnp.int32), pltpu.VMEM((2, rows, LANES), f32)],
        scratch_shapes=[pltpu.VMEM(slab, density.dtype), pltpu.VMEM((depth, columns), f32),
                        pltpu.VMEM((depth, columns), f32), pltpu.VMEM(color_table.shape, color_table.dtype),
                        pltpu.VMEM(opacity_table.shape, opacity_table.dtype), pltpu.SemaphoreType.DMA((CHUNKS + 2,))],
        compiler_params=pltpu.CompilerParams(vmem_limit_bytes=LIMIT),
        name="prepare",
    )(density, color_table, opacity_table)
    if halos is None:
        row_a = lax.ppermute(row_a, "narrow", pairs(8, 0))
        row_b = lax.ppermute(row_b, "narrow", pairs(8, 1))
        slice_a = lax.ppermute(slice_a, "wide", pairs(wide, 0))
        slice_b = lax.ppermute(slice_b, "wide", pairs(wide, 1))
    else:
        slice_a, slice_b, row_a, row_b = halos
    local = pl.pallas_call(
        functools.partial(lookup_kernel, depth_total=depth_total, place=place),
        in_specs=[smem, vmem, vmem, vmem],
        out_specs=[vmem] * 7,
        out_shape=[pltpu.VMEM((3,) + wider, f32), pltpu.VMEM(wider, f32), pltpu.VMEM(wider, f32), pltpu.VMEM(row, f32),
                   pltpu.VMEM(slab, f32), pltpu.VMEM(slab, f32), pltpu.VMEM(slab, f32)],
        scratch_shapes=[pltpu.VMEM(wider, f32), pltpu.VMEM(row, f32)],
        compiler_params=pltpu.CompilerParams(vmem_limit_bytes=LIMIT),
        cost_estimate=pl.CostEstimate(flops=30_000_000, bytes_accessed=10_000_000, transcendentals=0),
        name="lookup",
    )(view_shear, field, pair, mixed)
    bricks = pl.pallas_call(
        functools.partial(shade_kernel, depth_total=depth_total, place=place, across=across),
        in_specs=[smem] + [vmem] * 11,
        out_specs=vmem,
        out_shape=pltpu.VMEM((wide, rows, LANES), jnp.int16),
        scratch_shapes=[pltpu.VMEM(widest, f32), pltpu.VMEM(wider, f32), pltpu.VMEM((depth, columns), f32),
                        pltpu.VMEM((depth, columns), f32), pltpu.VMEM((3,) + row, f32), pltpu.VMEM((3,) + row, f32)],
        compiler_params=pltpu.CompilerParams(vmem_limit_bytes=LIMIT),
        name="shade",
    )(view_shear, *local, slice_a, slice_b, row_a, row_b)
    if halos is not None:
        return bricks
    order = [(i + TURN) % wide for i in range(wide)]
    parts = lax.all_to_all(bricks, "wide", split_axis=0, concat_axis=0, axis_index_groups=[order], tiled=True)
    return pl.pallas_call(
        merge_kernel,
        in_specs=[smem, vmem],
        out_specs=vmem,
        out_shape=jax.ShapeDtypeStruct((4, rows, 32), f32),
        name="merge",
    )(view_shear, parts)


def solution(mesh):
    placed = (P("wide", "narrow", None), P(), P(), P())
    return jax.shard_map(
        per_device, mesh=mesh, in_specs=placed, out_specs=P(None, "narrow", "wide"), check_vma=False
    )
```
